512 devices in a mesh: grp: 4 (over x_lo, core), tile: 128 (over x_hi, z, y).
Axes of the slice: x: 4 (x_hi: 2, x_lo: 2; x = x_hi * 2 + x_lo), y: 4, z: 16, core: 2. Of those that a mesh axis runs over, the one named last changes fastest.
Arguments:
- flow_state: float32 [4, 4, 512, 2048], P('grp', None, 'tile'), may hold values from -6 to 6
- line_owner: int32 [8192, 1], replicated, may hold values from 0 to 127; in each aligned block of 8192 rows (0 to 8191, 8192 to 16383, ...) at most 128 rows name the same one
Outputs:
- record: float32 [4, 128, 512, 128], P('grp', 'tile')
The draws below stay inside these ranges and needn't reach their ends.
Inputs may be any that keep to these rules, and one draw needn't show every extreme that they name: `line_owner`: no pencil owns more than 128 lines, some pencil owns exactly 128, and every pencil owns at least one line.
All inputs are finite; a program needn't handle non-finite values.
Results may differ from the reference program's by a relative error of at most 0.00002.
Values sent between devices are 32-bit elements; how exact they have to be, the bound alone decides.
No kernel may reach another device: no remote copies, remote signals or barrier semaphores. Data moves between devices by JAX's collectives and lax.ppermute only.
A program may use at most 64 MiB of HBM per device.

```python
import math
import jax
import jax.numpy as jnp
import numpy as np
from jax import lax

NY = 2048
PLANES = 4
NX = 512
NL = 8192
CAP = 128
N_GRP = 4
N_TILE = 128


def steps_of(rng, shape, shards, least, largest):
    loudness, own = 1.0, jax.random.fold_in(rng, 6)
    for dim, parts in shards:
        steps = jnp.exp(jax.random.uniform(jax.random.fold_in(own, dim), (parts,), jnp.float32, least / len(shards), largest / len(shards)))
        loudness = loudness * jnp.repeat(steps, shape[dim] // parts).reshape([-1 if axis == dim else 1 for axis in range(len(shape))])
    return loudness


def assign_block(rng, own, number, rows, amount, top, limit, skew):
    ranking = jax.random.permutation(rng, amount)
    crowded, ordinary = portions_of(amount, rows * top, limit, skew, True), portions_of(amount, rows * top, limit, skew, False)
    places = jnp.arange(amount)

    def named(tallies, offset_by):
        used = int((tallies > 0).sum())
        fixed = max(1, used // 4)
        moved = fixed + (places - fixed + offset_by * (used - fixed)) % max(1, amount - fixed)
        return jnp.zeros((amount,), jnp.int32).at[ranking[jnp.where(places < fixed, places, moved)]].set(jnp.asarray(tallies, jnp.int32))

    tallies = jnp.where(number % 4 == 0, named(crowded, number // 4), named(ordinary, number - number // 4 - 1))
    mixed = jax.random.permutation(jax.random.fold_in(own, 3), amount)
    giver, receiver = mixed[0:amount // 2 * 2:2], mixed[1:amount // 2 * 2:2]
    room = jnp.minimum(tallies[giver] - 1, limit - tallies[receiver]) // 2
    room = jnp.where((giver == ranking[0]) | (receiver == ranking[0]) | (tallies[receiver] == 0), 0, jnp.maximum(room, 0))
    moved = jax.random.randint(jax.random.fold_in(own, 4), (amount // 2,), 0, 1 << 20) % (room + 1)
    tallies = tallies.at[giver].add(-moved).at[receiver].add(moved)
    labels = jnp.searchsorted(jnp.cumsum(tallies), jnp.arange(rows * top), side="right").astype(jnp.int32)
    listing = labels.reshape(top, rows).T
    listing = listing[jax.random.permutation(jax.random.fold_in(own, 1), rows)]
    offset_by = jax.random.randint(jax.random.fold_in(own, 2), (rows, 1), 0, top)
    return jnp.take_along_axis(listing, (jnp.arange(top)[None, :] + offset_by) % top, axis=1)


def portions_of(count, total, bound, lean, full):
    loads = [(1 << 20) // math.isqrt(grade ** lean) + 1 for grade in range(1, count + 1)]
    largest = bound if full else min(bound, max(-(-total // count), total * loads[0] // sum(loads)))
    least = 1 if total - largest >= count - 1 else 0
    holding, rest = [largest] + [least] * (count - 1), total - largest - least * (count - 1)
    while rest > 0:
        movable = [i for i in range(1, count) if holding[i] < largest] or [i for i in range(1, count) if holding[i] < bound]
        pool, remaining = sum([loads[i] for i in movable]), rest
        for i in movable:
            addition = min(bound - holding[i], max(1, remaining * loads[i] // pool), rest)
            holding[i] = holding[i] + addition
            rest = rest - addition
    return np.array(holding)


def centred(key, dims, scale, reach, pieces=(), kind=jnp.bfloat16):
    factor_of = steps_of(key, dims, pieces, -0.22, 0.18) if pieces else 1.0
    array = jax.random.normal(key, dims, jnp.float32) * scale * factor_of
    return jnp.minimum(jnp.maximum(array, -reach), reach).astype(kind)


def setup_inputs(seed: int = 0) -> dict:
    key_list = jax.random.split(jax.random.key(seed), 3)
    flow_state = centred(key_list[0], (N_GRP, PLANES, NX, NY), 1.0, 6.0, ((0, 4), (2, 128)), jnp.float32)
    line_owner_keys = jax.random.split(jax.random.fold_in(key_list[1], 1), NL // NL)
    line_owner_turns = jax.random.permutation(jax.random.fold_in(key_list[1], 3), NL // NL)
    line_owner = jax.vmap(lambda own, number: assign_block(jax.random.fold_in(key_list[1], 2), own, number, NL, N_TILE, 1, CAP, 2))(line_owner_keys, line_owner_turns).reshape((NL, 1))
    return {"flow_state": flow_state, "line_owner": line_owner}


time_step = 0.2
viscosity = 0.05
first_coeffs = (0.8, -0.2, 4.0 / 105.0, -1.0 / 280.0)
second_center = -205.0 / 72.0
second_coeffs = (1.6, -0.2, 8.0 / 315.0, -1.0 / 560.0)
lift_alpha = -1.586134342059924
lift_beta = -0.052980118572961
lift_gamma = 0.882911075530934
lift_delta = 0.443506852043971
lift_scale = 1.149604398860241


def first_rolled(field_now, along_axis):
    running = jnp.zeros_like(field_now)
    for offset in range(4):
        forward = jnp.roll(field_now, -(offset + 1), along_axis)
        behind = jnp.roll(field_now, offset + 1, along_axis)
        running = running + first_coeffs[offset] * (forward - behind)
    return running


def second_rolled(field_now, along_axis):
    running = second_center * field_now
    for offset in range(4):
        forward = jnp.roll(field_now, -(offset + 1), along_axis)
        behind = jnp.roll(field_now, offset + 1, along_axis)
        running = running + second_coeffs[offset] * (forward + behind)
    return running


def tendencies(fields):
    pressure = fields[3]
    grad_axes = (1, 2, 0)
    result = []
    for component in range(3):
        field_now = fields[component]
        advect = fields[0] * first_rolled(field_now, 1) + fields[1] * first_rolled(field_now, 2) + fields[2] * first_rolled(field_now, 0)
        laplace = second_rolled(field_now, 1) + second_rolled(field_now, 2) + second_rolled(field_now, 0)
        result.append(-advect - first_rolled(pressure, grad_axes[component]) + viscosity * laplace)
    return jnp.stack(result)


def lift_axis(signal, along_axis):
    length = signal.shape[along_axis]
    even_part = lax.slice_in_dim(signal, 0, length, 2, along_axis)
    odd_part = lax.slice_in_dim(signal, 1, length, 2, along_axis)
    odd_part = odd_part + lift_alpha * (even_part + jnp.roll(even_part, -1, along_axis))
    even_part = even_part + lift_beta * (odd_part + jnp.roll(odd_part, 1, along_axis))
    odd_part = odd_part + lift_gamma * (even_part + jnp.roll(even_part, -1, along_axis))
    even_part = even_part + lift_delta * (odd_part + jnp.roll(odd_part, 1, along_axis))
    return jnp.concatenate([even_part * lift_scale, odd_part / lift_scale], along_axis)


def line_slots(line_owner, pencils, capacity):
    owners = line_owner[:, 0].astype(jnp.int32)
    sorted_lines = jnp.argsort(owners, stable=True).astype(jnp.int32)
    sorted_owner = owners[sorted_lines]
    targets = jnp.arange(pencils, dtype=jnp.int32)
    starts = jnp.searchsorted(sorted_owner, targets, side="left").astype(jnp.int32)
    ends_at = jnp.searchsorted(sorted_owner, targets, side="right").astype(jnp.int32)
    counts = ends_at - starts
    slot_index = jnp.arange(capacity, dtype=jnp.int32)
    position = jnp.minimum(starts[:, None] + slot_index[None, :], owners.shape[0] - 1)
    chosen = sorted_lines[position]
    usable = slot_index[None, :] < counts[:, None]
    return chosen, usable


def reference(flow_state, line_owner):
    velocity = flow_state[:3]
    pressure = flow_state[3:]
    middle = velocity + time_step * tendencies(flow_state)
    finished = 0.5 * ((velocity + middle) + time_step * tendencies(jnp.concatenate([middle, pressure], 0)))
    coeffs = lift_axis(lift_axis(lift_axis(finished, 3), 1), 2)
    planes = coeffs.shape[1]
    line_table = jnp.transpose(coeffs, (0, 1, 3, 2)).reshape(3, planes * coeffs.shape[3], coeffs.shape[2])
    chosen, usable = line_slots(line_owner, N_TILE, CAP)
    picked = jnp.take(line_table, chosen.reshape(-1), axis=1).reshape(3, N_TILE, CAP, line_table.shape[2])
    picked = jnp.where(usable[None, :, :, None], picked, 0.0)
    record = jnp.transpose(picked, (0, 1, 3, 2))
    energy = record[0] * record[0] + record[1] * record[1] + record[2] * record[2]
    return jnp.concatenate([record, energy[None]], 0)
```

```python
import jax
import jax.numpy as jnp
from jax import lax
from jax.experimental import pallas as pl
from jax.experimental.pallas import tpu as pltpu
from jax.sharding import Mesh
from jax.sharding import PartitionSpec as P

BLOCK_AXES = ("y", "xl", "co")
LONG_AXES = ("xh", "z")

time_step = 0.2
viscosity = 0.05
first_coeffs = (0.8, -0.2, 4.0 / 105.0, -1.0 / 280.0)
second_center = -205.0 / 72.0
second_coeffs = (1.6, -0.2, 8.0 / 315.0, -1.0 / 560.0)
lift_alpha = -1.586134342059924
lift_beta = -0.052980118572961
lift_gamma = 0.882911075530934
lift_delta = 0.443506852043971
lift_scale = 1.149604398860241

PLANES = 4
CHUNKS = 16
VMEM_LIMIT = 48 * 1024 * 1024


def lanes_of(shape):
    return lax.broadcasted_iota(jnp.int32, shape, len(shape) - 1)


def whole(count):
    return [pl.BlockSpec(memory_space=pltpu.VMEM)] * count


def cost(flops, moved):
    return pl.CostEstimate(flops=flops, bytes_accessed=moved, transcendentals=0)


def pack_kernel(x_ref, out_ref):
    lane = lanes_of((8, 128))
    for c in range(CHUNKS):
        here = slice(128 * c, 128 * c + 128)
        after = slice(128 * ((c + 1) % CHUNKS), 128 * ((c + 1) % CHUNKS) + 128)
        before = slice(128 * ((c - 1) % CHUNKS), 128 * ((c - 1) % CHUNKS) + 128)
        for z in range(PLANES):
            out_ref[c, 4 * z : 4 * z + 4, :] = x_ref[z, :, here]
        right_a = jnp.concatenate([x_ref[0, :, after], x_ref[1, :, after]], 0)
        right_b = jnp.concatenate([x_ref[2, :, after], x_ref[3, :, after]], 0)
        left_a = jnp.concatenate([x_ref[0, :, before], x_ref[1, :, before]], 0)
        left_b = jnp.concatenate([x_ref[2, :, before], x_ref[3, :, before]], 0)
        right = jnp.where(lane < 32, right_a, pltpu.roll(right_b, 32, 1))
        left = jnp.where(lane < 96, pltpu.roll(left_b, 96, 1), left_a)
        out_ref[c, 16:24, :] = jnp.where(lane < 64, right, left)


def pack(x):
    return pl.pallas_call(
        pack_kernel,
        out_shape=jax.ShapeDtypeStruct((CHUNKS, 24, 128), jnp.float32),
        in_specs=whole(1),
        out_specs=whole(1)[0],
        cost_estimate=cost(100_000, 320_000),
        name="pack",
    )(x)


def derivatives(ref, f, z, rows, low):
    here = ref[f, z, low : low + rows, :]
    d_x = d_y = d_z = None
    lap = (3.0 * second_center) * here
    for k in range(1, 5):
        a, e = first_coeffs[k - 1], second_coeffs[k - 1]
        up, down = ref[f, z, low + k : low + k + rows, :], ref[f, z, low - k : low - k + rows, :]
        right, left = pltpu.roll(here, 256 - k, 1), pltpu.roll(here, k, 1)
        over, under = ref[f, (z + k) % 4, low : low + rows, :], ref[f, (z - k) % 4, low : low + rows, :]
        t_x, t_y, t_z = a * (up - down), a * (right - left), a * (over - under)
        d_x = t_x if d_x is None else d_x + t_x
        d_y = t_y if d_y is None else d_y + t_y
        d_z = t_z if d_z is None else d_z + t_z
        lap = lap + e * ((up + down) + (right + left) + (over + under))
    return d_x, d_y, d_z, lap


def pressure_slopes(ref, z, rows, low):
    here = ref[3, z, low : low + rows, :]
    d_x = d_y = d_z = None
    for k in range(1, 5):
        a = first_coeffs[k - 1]
        t_x = a * (ref[3, z, low + k : low + k + rows, :] - ref[3, z, low - k : low - k + rows, :])
        t_y = a * (pltpu.roll(here, 256 - k, 1) - pltpu.roll(here, k, 1))
        t_z = a * (ref[3, (z + k) % 4, low : low + rows, :] - ref[3, (z - k) % 4, low : low + rows, :])
        d_x = t_x if d_x is None else d_x + t_x
        d_y = t_y if d_y is None else d_y + t_y
        d_z = t_z if d_z is None else d_z + t_z
    return d_x, d_y, d_z


def lift_steps(s, odd, axis):
    size = s.shape[axis]
    for coeff, on_odd in ((lift_alpha, True), (lift_beta, False), (lift_gamma, True), (lift_delta, False)):
        step = coeff * (pltpu.roll(s, 1, axis) + pltpu.roll(s, size - 1, axis))
        s = jnp.where(odd == on_odd, s + step, s)
    return s


def flow_kernel(own_ref, low_ref, high_ref, out_ref, fields, middle, lifted):
    lane8 = lanes_of((8, 128))
    for ref, count, base in ((low_ref, 3, 0), (own_ref, 4, 12), (high_ref, 3, 28)):
        for j in range(count):
            for g in range(4):
                block = ref[4 * j + g]
                near = block[16:24]
                far = jnp.where(lane8 < 64, pltpu.roll(near, 96, 1), pltpu.roll(near, 32, 1))
                for z in range(PLANES):
                    rows = slice(base + 4 * j, base + 4 * j + 4)
                    sides = near if z < 2 else far
                    fields[g, z, rows, 0:128] = block[4 * z : 4 * z + 4]
                    fields[g, z, rows, 128:256] = sides[4 * (z % 2) : 4 * (z % 2) + 4]

    for z in range(PLANES):
        slopes = pressure_slopes(fields, z, 32, 4)
        u, v, w = (fields[f, z, 4:36, :] for f in range(3))
        for g in range(3):
            d_x, d_y, d_z, lap = derivatives(fields, g, z, 32, 4)
            tend = viscosity * lap - (u * d_x + v * d_y + w * d_z) - slopes[g]
            middle[g, z, :, :] = (u, v, w)[g] + time_step * tend

    odd_lane = lanes_of((24, 256)) % 2 == 1
    for z in range(PLANES):
        slopes = pressure_slopes(fields, z, 24, 8)
        u, v, w = (middle[f, z, 4:28, :] for f in range(3))
        for g in range(3):
            d_x, d_y, d_z, lap = derivatives(middle, g, z, 24, 4)
            tend = viscosity * lap - (u * d_x + v * d_y + w * d_z) - slopes[g]
            done = 0.5 * ((fields[g, z, 8:32, :] + (u, v, w)[g]) + time_step * tend)
            lifted[g, z, :, :] = lift_steps(done, odd_lane, 1)[:, 0:128]

    odd_row = lax.broadcasted_iota(jnp.int32, (24, 128), 0) % 2 == 1
    for g in range(3):
        even0, odd0, even1, odd1 = (lifted[g, z, :, :] for z in range(PLANES))
        both = lift_alpha * (even0 + even1)
        odd0, odd1 = odd0 + both, odd1 + both
        both = lift_beta * (odd0 + odd1)
        even0, even1 = even0 + both, even1 + both
        both = lift_gamma * (even0 + even1)
        odd0, odd1 = odd0 + both, odd1 + both
        both = lift_delta * (odd0 + odd1)
        even0, even1 = even0 + both, even1 + both
        for z, plane in enumerate((even0, odd0, even1, odd1)):
            lifted[g, z, :, :] = lift_steps(plane, odd_row, 0)

    odd_lane = lanes_of((8, 128)) % 2 == 1
    for z in range(PLANES):
        for half in range(2):
            power = (-1 if z % 2 else 1) + (-1 if half else 1)
            scale = jnp.where(odd_lane, lift_scale ** (power - 1), lift_scale ** (power + 1)).astype(jnp.float32)
            energy = None
            for g in range(3):
                rows = lifted[g, z, pl.ds(4 + half, 8, stride=2), :] * scale
                energy = rows * rows if energy is None else energy + rows * rows
                for copy in range(4):
                    out_ref[copy, g, z, 8 * half : 8 * half + 8, :] = rows
            for copy in range(4):
                out_ref[copy, 3, z, 8 * half : 8 * half + 8, :] = energy


def flow(own, low, high):
    return pl.pallas_call(
        flow_kernel,
        out_shape=jax.ShapeDtypeStruct((4, 4, PLANES, 16, 128), jnp.float32),
        in_specs=whole(3),
        out_specs=whole(1)[0],
        scratch_shapes=[
            pltpu.VMEM((4, PLANES, 40, 256), jnp.float32),
            pltpu.VMEM((3, PLANES, 32, 256), jnp.float32),
            pltpu.VMEM((3, PLANES, 24, 128), jnp.float32),
        ],
        compiler_params=pltpu.CompilerParams(vmem_limit_bytes=VMEM_LIMIT),
        cost_estimate=cost(30_000_000, 1_000_000),
        name="flow",
    )(own, low, high)


def slots_kernel(owner_ref, owner_out, rank_out, rank_rows):
    bf16, f32 = jnp.bfloat16, jnp.float32
    row = lax.broadcasted_iota(jnp.int32, (128, 128), 0)
    lane = lanes_of((128, 128))
    before = jnp.concatenate([(row < lane).astype(f32), jnp.ones((128, 128), f32)], 1).astype(bf16)
    pencil = row
    base = jnp.zeros((128, 128), f32)
    for b in range(64):
        mine = owner_ref[b : b + 1, :] == pencil
        counts = jnp.dot(jnp.where(mine, 1.0, 0.0).astype(bf16), before, preferred_element_type=f32)
        ranks = jnp.where(mine, base + counts[:, 0:128], 0.0)
        rank_rows[b : b + 1, :] = jnp.sum(ranks, axis=0, keepdims=True)
        base = base + counts[:, 128:256]
    owners = owner_ref[...].astype(f32).astype(bf16)
    ranks = rank_rows[...].astype(bf16)
    for part in range(2):
        even = jnp.where(lane == 2 * (row - 64 * part), 1.0, 0.0).astype(bf16)
        odd = jnp.where(lane == 2 * (row - 64 * part) + 1, 1.0, 0.0).astype(bf16)
        for values, out in ((owners, owner_out), (ranks, rank_out)):
            from_even = jnp.dot(values, even, preferred_element_type=f32)
            from_odd = jnp.dot(values, odd, preferred_element_type=f32)
            for z in range(PLANES):
                plane = (0, 2, 1, 3)[z]
                low = from_even[16 * plane : 16 * plane + 8]
                high = from_odd[16 * plane + 8 : 16 * plane + 16]
                out[part, z, :, :] = (low + high).astype(jnp.int32)


def slots(owner_rows):
    shape = jax.ShapeDtypeStruct((2, PLANES, 8, 128), jnp.int32)
    return pl.pallas_call(
        slots_kernel,
        out_shape=(shape, shape),
        in_specs=whole(1),
        out_specs=tuple(whole(2)),
        scratch_shapes=[pltpu.VMEM((64, 128), jnp.float32)],
        compiler_params=pltpu.CompilerParams(vmem_limit_bytes=VMEM_LIMIT),
        cost_estimate=cost(600_000_000, 100_000),
        name="slots",
    )(owner_rows)


def gather_kernel(first_ref, table_ref, owner_ref, rank_ref, out_ref, left):
    bf16, f32 = jnp.bfloat16, jnp.float32
    first = first_ref[0]
    slot = lax.broadcasted_iota(jnp.int32, (128, 128), 0)
    out_ref[...] = jnp.zeros_like(out_ref)

    def chunk(c, carry):
        right = []
        for z in range(PLANES):
            values = table_ref[c, z]
            high = values.astype(bf16).astype(f32)
            low = values - high
            owner = jnp.broadcast_to(owner_ref[c % 2, z, pl.ds(c // 2, 1), :], (16, 128)) - first
            for t in range(32):
                mine = owner == 4 * t
                rows = slice(16 * t, 16 * t + 16)
                left[rows, 256 * z : 256 * z + 128] = jnp.where(mine, high, 0.0).astype(bf16)
                left[rows, 256 * z + 128 : 256 * z + 256] = jnp.where(mine, low, 0.0).astype(bf16)
            rank = rank_ref[c % 2, z, pl.ds(c // 2, 1), :]
            at = jnp.where(rank == slot, 1.0, 0.0).astype(bf16)
            right += [at, at]
        moved = lax.dot_general(
            left[...], jnp.concatenate(right, 1), (((1,), (1,)), ((), ())), preferred_element_type=f32
        )
        out_ref[...] += moved.reshape(32, 16, 128)
        return carry

    lax.fori_loop(0, CHUNKS, chunk, 0)


def gather(first, table, owner, rank):
    return pl.pallas_call(
        gather_kernel,
        out_shape=jax.ShapeDtypeStruct((32, 16, 128), jnp.float32),
        in_specs=[pl.BlockSpec(memory_space=pltpu.SMEM)] + whole(3),
        out_specs=whole(1)[0],
        scratch_shapes=[pltpu.VMEM((512, 1024), jnp.bfloat16)],
        compiler_params=pltpu.CompilerParams(vmem_limit_bytes=VMEM_LIMIT),
        cost_estimate=cost(2_200_000_000, 1_000_000),
        name="gather",
    )(first, table, owner, rank)


def swap(x, axes):
    return lax.all_to_all(x, axes, split_axis=0, concat_axis=0, tiled=True)


def body(flow_state, line_owner):
    owner, rank = slots(line_owner.reshape(64, 128))
    own = swap(pack(flow_state[0]), BLOCK_AXES)
    blocks = lax.axis_size(LONG_AXES)
    up = [(i, (i + 1) % blocks) for i in range(blocks)]
    low = lax.ppermute(own[4:16], LONG_AXES, up)
    high = lax.ppermute(own[0:12], LONG_AXES, [(b, a) for a, b in up])
    coeffs = flow(own, low, high).reshape(16, PLANES, 16, 128)
    table = swap(coeffs, BLOCK_AXES)
    first = lax.axis_index("y").astype(jnp.int32).reshape(1)
    outgoing = gather(first, table, owner, rank)
    record = swap(outgoing, LONG_AXES)
    record = record.reshape(32, 2, 8, 128).transpose(1, 0, 2, 3).reshape(512, 128)
    return record[None, None]


def solution(mesh):
    split = Mesh(mesh.devices.reshape(2, 2, 2, 16, 4), ("xl", "co", "xh", "z", "y"))
    in_specs = (P(("xl", "co"), None, ("xh", "z", "y"), None), P())
    out_specs = P(("xl", "co"), ("xh", "z", "y"), None, None)
    return jax.shard_map(body, mesh=split, in_specs=in_specs, out_specs=out_specs, check_vma=False)
```

```python
import jax
import jax.numpy as jnp
from jax import lax
from jax.experimental import pallas as pl
from jax.experimental.pallas import tpu as pltpu
from jax.sharding import Mesh
from jax.sharding import PartitionSpec as P

BLOCK_AXES = ("y", "xl", "co")
LONG_AXES = ("xh", "z")

time_step = 0.2
viscosity = 0.05
first_coeffs = (0.8, -0.2, 4.0 / 105.0, -1.0 / 280.0)
second_center = -205.0 / 72.0
second_coeffs = (1.6, -0.2, 8.0 / 315.0, -1.0 / 560.0)
lift_alpha = -1.586134342059924
lift_beta = -0.052980118572961
lift_gamma = 0.882911075530934
lift_delta = 0.443506852043971
lift_scale = 1.149604398860241

PLANES = 4
CHUNKS = 16
VMEM_LIMIT = 24 * 1024 * 1024


def lanes_of(shape):
    return lax.broadcasted_iota(jnp.int32, shape, len(shape) - 1)


def whole(count):
    return [pl.BlockSpec(memory_space=pltpu.VMEM)] * count


def cost(flops, moved):
    return pl.CostEstimate(flops=flops, bytes_accessed=moved, transcendentals=0)


def pack_kernel(x_ref, out_ref):
    right_lane = lanes_of((4, 128)) < 64
    for r in range(4):
        chunks = [x_ref[:, r, 128 * c : 128 * c + 128] for c in range(CHUNKS)]
        for c in range(CHUNKS):
            out_ref[c, r, 0:4, :] = chunks[c]
            out_ref[c, r, 4:8, :] = jnp.where(right_lane, chunks[(c + 1) % CHUNKS], chunks[c - 1])


def pack(x):
    return pl.pallas_call(
        pack_kernel,
        out_shape=pltpu.VMEM((CHUNKS, 4, 8, 128), jnp.float32),
        in_specs=whole(1),
        out_specs=whole(1)[0],
        cost_estimate=cost(100_000, 400_000),
        name="pack",
    )(x)


def folded(coeffs, sign):
    weights = [0.0] * PLANES
    for k, value in enumerate(coeffs, 1):
        weights[k % PLANES] += value
        weights[-k % PLANES] += sign * value
    return weights


def column_shifts(here, lane, reach):
    other = pltpu.roll(here, 4, 1)
    right = [pltpu.roll(jnp.where(lane < k, other, here), 128 - k, 2) for k in range(1, reach + 1)]
    left = [pltpu.roll(jnp.where(lane >= 128 - k, other, here), k, 2) for k in range(1, reach + 1)]
    return right, left


def plane_shifts(here, plane):
    over = jnp.where(plane < 3, pltpu.roll(here, 7, 1), pltpu.roll(here, 3, 1))
    under = jnp.where(plane > 0, pltpu.roll(here, 1, 1), pltpu.roll(here, 5, 1))
    return over, under


def plane_opposite(here, plane):
    return jnp.where(plane < 2, pltpu.roll(here, 6, 1), pltpu.roll(here, 2, 1))


def weighted(coeffs, terms):
    total = None
    for value, term in zip(coeffs, terms):
        total = value * term if total is None else total + value * term
    return total


def derivatives(load, low, lane, plane, second=True):
    here = load(low)
    right, left = column_shifts(here, lane, 4)
    up, down = ([load(low + s * k) for k in range(1, 5)] for s in (1, -1))
    over, under = plane_shifts(here, plane)
    _, forward, _, behind = folded(first_coeffs, -1.0)
    assert forward == -behind
    d_x = weighted(first_coeffs, [a - b for a, b in zip(up, down)])
    d_y = weighted(first_coeffs, [a - b for a, b in zip(right, left)])
    d_z = forward * (over - under)
    if not second:
        return d_x, d_y, d_z
    centre, near, far, _ = folded(second_coeffs, 1.0)
    lap = weighted(second_coeffs, [(a + b) + (c + d) for a, b, c, d in zip(up, down, right, left)])
    lap = lap + (3.0 * second_center + centre) * here
    lap = lap + (near * (over + under) + far * plane_opposite(here, plane))
    return d_x, d_y, d_z, lap


def flow_kernel(own_ref, low_ref, high_ref, out_ref, fields, middle, slopes, lifted):
    for ref, count, base in ((low_ref, 3, 0), (own_ref, 4, 12), (high_ref, 3, 28)):
        for j in range(count):
            for g in range(4):
                fields[g, base + 4 * j : base + 4 * j + 4] = ref[4 * j + g]

    shape = (4, 8, 128)
    lane = lanes_of(shape)
    plane = lax.broadcasted_iota(jnp.int32, shape, 1) % 4

    def loader(ref, g):
        return lambda low: ref[g, pl.ds(low, 4)]

    def first(i, carry):
        low = 4 + 4 * i
        grads = derivatives(loader(fields, 3), low, lane, plane, second=False)
        u, v, w = (fields[f, pl.ds(low, 4)] for f in range(3))
        for g in range(3):
            d_x, d_y, d_z, lap = derivatives(loader(fields, g), low, lane, plane)
            slopes[g, pl.ds(4 * i, 4)] = grads[g]
            tend = viscosity * lap - (u * d_x + v * d_y + w * d_z) - grads[g]
            middle[g, pl.ds(4 * i, 4)] = (u, v, w)[g] + time_step * tend
        return carry

    lax.fori_loop(0, 8, first, 0)

    def second(i, carry):
        low = 4 + 4 * i
        u, v, w = (middle[f, pl.ds(low, 4)] for f in range(3))
        for g in range(3):
            d_x, d_y, d_z, lap = derivatives(loader(middle, g), low, lane, plane)
            tend = viscosity * lap - (u * d_x + v * d_y + w * d_z) - slopes[g, pl.ds(low, 4)]
            s = 0.5 * ((fields[g, pl.ds(low + 4, 4)] + (u, v, w)[g]) + time_step * tend)
            lifted[g, pl.ds(4 * i, 4)] = s
        return carry

    lax.fori_loop(0, 6, second, 0)

    lane, sub = lanes_of((8, 128)), lax.broadcasted_iota(jnp.int32, (8, 128), 0)
    odd_y, odd_z, first_row = lane % 2 == 1, sub % 2 == 1, sub < 4

    def chosen(odd, pair):
        return jnp.where(odd, jnp.float32(pair[1]), jnp.float32(pair[0]))

    taps = [chosen(odd_y, pair) for pair in filter_taps(None)]
    same, opposite = (chosen(odd_z, pair) for pair in filter_taps(PLANES))
    energy = [None] * 8
    for g in range(3):
        even = [lifted[g, 2 * i] for i in range(12)]
        odd = [lifted[g, 2 * i + 1] for i in range(12)]
        odd = [o + lift_alpha * (even[i] + even[i + 1]) for i, o in enumerate(odd[:11])]
        even = [None] + [even[i] + lift_beta * (odd[i] + odd[i - 1]) for i in range(1, 11)]
        odd = [None] + [odd[i] + lift_gamma * (even[i] + even[i + 1]) for i in range(1, 10)]
        even = [None, None] + [even[i] + lift_delta * (odd[i] + odd[i - 1]) for i in range(2, 10)]
        for pair in range(8):
            a, b = (even, odd)[pair // 4][2 + 2 * (pair % 4) : 4 + 2 * (pair % 4)]
            here = jnp.where(first_row, a, pltpu.roll(b, 4, 0))
            around = jnp.where(first_row, pltpu.roll(a, 4, 0), b)
            rows = taps[0] * here
            for k in range(1, 5):
                right = pltpu.roll(jnp.where(lane < k, around, here), 128 - k, 1)
                left = pltpu.roll(jnp.where(lane >= 128 - k, around, here), k, 1)
                rows = rows + taps[k] * (right + left)
            both = rows + jnp.where(sub % 4 < 2, pltpu.roll(rows, 6, 0), pltpu.roll(rows, 2, 0))
            others = jnp.where(odd_z, pltpu.roll(both, 1, 0), pltpu.roll(both, 7, 0))
            rows = rows + (same * both + opposite * others)
            scale = chosen(odd_z, (lift_scale, 1.0 / lift_scale)) * (lift_scale if pair < 4 else 1.0 / lift_scale)
            rows = rows * scale
            energy[pair] = rows * rows if g == 0 else energy[pair] + rows * rows
            for copy in range(4):
                out_ref[4 * copy + g, 8 * pair : 8 * pair + 8, :] = rows
    for pair in range(8):
        for copy in range(4):
            out_ref[4 * copy + 3, 8 * pair : 8 * pair + 8, :] = energy[pair]


def filter_taps(ring):
    size = ring or 32

    def lifted(s):
        for value, start in ((lift_alpha, 1), (lift_beta, 0), (lift_gamma, 1), (lift_delta, 0)):
            s = list(s)
            for i in range(start, size, 2):
                s[i] += value * (s[i - 1] + s[(i + 1) % size])
        return s

    answers = [lifted([1.0 if i == j else 0.0 for i in range(size)]) for j in range(size)]
    if ring:
        return tuple(tuple(answers[(i + d) % size][i] - (0.0 if d else 1.0) for i in (0, 1)) for d in (0, 1))
    scales = (lift_scale, 1.0 / lift_scale)
    return [tuple(answers[16 + odd + k][16 + odd] * scales[odd] for odd in (0, 1)) for k in range(5)]


def flow(own, low, high):
    return pl.pallas_call(
        flow_kernel,
        out_shape=pltpu.VMEM((16, 64, 128), jnp.float32),
        in_specs=whole(3),
        out_specs=whole(1)[0],
        scratch_shapes=[
            pltpu.VMEM((4, 40, 8, 128), jnp.float32),
            pltpu.VMEM((3, 32, 8, 128), jnp.float32),
            pltpu.VMEM((3, 32, 8, 128), jnp.float32),
            pltpu.VMEM((3, 24, 8, 128), jnp.float32),
        ],
        compiler_params=pltpu.CompilerParams(vmem_limit_bytes=VMEM_LIMIT),
        cost_estimate=cost(30_000_000, 1_000_000),
        name="flow",
    )(own, low, high)


def slots_kernel(owner_ref, owner_out, rank_out, rank_rows):
    bf16, f32 = jnp.bfloat16, jnp.float32
    row = lax.broadcasted_iota(jnp.int32, (128, 128), 0)
    lane = lanes_of((128, 128))
    before = jnp.concatenate([(row < lane).astype(f32), jnp.ones((128, 128), f32)], 1).astype(bf16)
    pencil = row
    base = jnp.zeros((128, 128), f32)
    for b in range(64):
        mine = owner_ref[b : b + 1, :] == pencil
        counts = jnp.dot(jnp.where(mine, 1.0, 0.0).astype(bf16), before, preferred_element_type=f32)
        ranks = jnp.where(mine, base + counts[:, 0:128], 0.0)
        rank_rows[b : b + 1, :] = jnp.sum(ranks, axis=0, keepdims=True)
        base = base + counts[:, 128:256]
    owners = owner_ref[...].astype(f32).astype(bf16)
    ranks = rank_rows[...].astype(bf16)
    for part in range(2):
        even = jnp.where(lane == 2 * (row - 64 * part), 1.0, 0.0).astype(bf16)
        odd = jnp.where(lane == 2 * (row - 64 * part) + 1, 1.0, 0.0).astype(bf16)
        for values, out in ((owners, owner_out), (ranks, rank_out)):
            from_even = jnp.dot(values, even, preferred_element_type=f32)
            from_odd = jnp.dot(values, odd, preferred_element_type=f32)
            for z in range(PLANES):
                plane = (0, 2, 1, 3)[z]
                low = from_even[16 * plane : 16 * plane + 8]
                high = from_odd[16 * plane + 8 : 16 * plane + 16]
                out[part, z, :, :] = (low + high).astype(jnp.int32)


def slots(owner_rows):
    shape = jax.ShapeDtypeStruct((2, PLANES, 8, 128), jnp.int32)
    return pl.pallas_call(
        slots_kernel,
        out_shape=(shape, shape),
        in_specs=whole(1),
        out_specs=tuple(whole(2)),
        scratch_shapes=[pltpu.VMEM((64, 128), jnp.float32)],
        compiler_params=pltpu.CompilerParams(vmem_limit_bytes=VMEM_LIMIT),
        cost_estimate=cost(600_000_000, 100_000),
        name="slots",
    )(owner_rows)


def gather_kernel(first_ref, table_ref, owner_ref, rank_ref, out_ref):
    bf16, f32 = jnp.bfloat16, jnp.float32
    first = first_ref[0]
    slot = lax.broadcasted_iota(jnp.int32, (256, 128), 0).astype(f32).astype(bf16)
    nothing = jnp.zeros((16, 128), bf16)

    def spread(row, rows):
        return jnp.broadcast_to(row, (rows, 128)).astype(f32).astype(bf16)

    def chunk(c, carry):
        moved = None
        for z in range(PLANES):
            values = table_ref[c, pl.ds(z, 16, stride=4), :]
            high = values.astype(bf16)
            low = (values - high.astype(f32)).astype(bf16)
            owner = owner_ref[c % 2, z, pl.ds(c // 2, 1), :]
            rank = rank_ref[c % 2, z, pl.ds(c // 2, 1), :]
            mine = owner % 4 == first
            pencil = owner // 4
            lower = spread(jnp.where(mine, pencil % 16, -1), 16)
            at = spread(jnp.where(mine, 128 * (pencil // 16) + rank, -1), 16)
            left = []
            for t in range(16):
                hit = lower == jnp.asarray(t, bf16)
                left.append(jnp.concatenate([jnp.where(hit, high, nothing), jnp.where(hit, low, nothing)], 1))
            ones = jnp.ones((16, 128), bf16)
            right = [jnp.where(at == slot[16 * k : 16 * k + 16], ones, nothing) for k in range(16)]
            right = jnp.concatenate(right, 0)
            part = lax.dot_general(
                jnp.concatenate(left, 0),
                jnp.concatenate([right, right], 1),
                (((1,), (1,)), ((), ())),
                preferred_element_type=f32,
            )
            moved = part if moved is None else moved + part
        for upper in range(2):
            part = moved[:, 128 * upper : 128 * upper + 128].reshape(16, 16, 128)
            rows = slice(16 * upper, 16 * upper + 16)
            out_ref[rows] = jnp.where(c == 0, part, out_ref[rows] + part)
        return carry

    lax.fori_loop(0, CHUNKS, chunk, 0, unroll=4)


def gather(first, table, owner, rank):
    return pl.pallas_call(
        gather_kernel,
        out_shape=jax.ShapeDtypeStruct((32, 16, 128), jnp.float32),
        in_specs=[pl.BlockSpec(memory_space=pltpu.SMEM)] + whole(3),
        out_specs=whole(1)[0],
        compiler_params=pltpu.CompilerParams(vmem_limit_bytes=VMEM_LIMIT),
        cost_estimate=cost(2_200_000_000, 1_000_000),
        name="gather",
    )(first, table, owner, rank)


def swap(x, axes):
    return lax.all_to_all(x, axes, split_axis=0, concat_axis=0, tiled=True)


def body(flow_state, line_owner):
    own = swap(pack(flow_state[0]), BLOCK_AXES)
    blocks = lax.axis_size(LONG_AXES)
    up = [(i, (i + 1) % blocks) for i in range(blocks)]
    own, lines = lax.optimization_barrier((own, line_owner.reshape(64, 128)))
    low = lax.ppermute(own[4:16], LONG_AXES, up)
    high = lax.ppermute(own[0:12], LONG_AXES, [(b, a) for a, b in up])
    owner, rank = slots(lines)
    own, owner, rank = lax.optimization_barrier((own, owner, rank))
    table = swap(flow(own, low, high), BLOCK_AXES)
    first = lax.axis_index("y").astype(jnp.int32).reshape(1)
    outgoing = gather(first, table, owner, rank)
    record = swap(outgoing, LONG_AXES)
    record = record.reshape(32, 2, 8, 128).transpose(1, 0, 2, 3).reshape(512, 128)
    return record[None, None]


def solution(mesh):
    split = Mesh(mesh.devices.reshape(2, 2, 2, 16, 4), ("xl", "co", "xh", "z", "y"))
    in_specs = (P(("xl", "co"), None, ("xh", "z", "y"), None), P())
    out_specs = P(("xl", "co"), ("xh", "z", "y"), None, None)
    return jax.shard_map(body, mesh=split, in_specs=in_specs, out_specs=out_specs, check_vma=False)
```

```python
import jax
import jax.numpy as jnp
from jax import lax
from jax.experimental import pallas as pl
from jax.experimental.pallas import tpu as pltpu
from jax.sharding import Mesh
from jax.sharding import PartitionSpec as P

BLOCK_AXES = ("y", "xl", "co")
LONG_AXES = ("xh", "z")

time_step = 0.2
viscosity = 0.05
first_coeffs = (0.8, -0.2, 4.0 / 105.0, -1.0 / 280.0)
second_center = -205.0 / 72.0
second_coeffs = (1.6, -0.2, 8.0 / 315.0, -1.0 / 560.0)
lift_alpha = -1.586134342059924
lift_beta = -0.052980118572961
lift_gamma = 0.882911075530934
lift_delta = 0.443506852043971
lift_scale = 1.149604398860241

PLANES = 4
CHUNKS = 16
VMEM_LIMIT = 24 * 1024 * 1024


def lanes_of(shape):
    return lax.broadcasted_iota(jnp.int32, shape, len(shape) - 1)


def whole(count):
    return [pl.BlockSpec(memory_space=pltpu.VMEM)] * count


def cost(flops, moved):
    return pl.CostEstimate(flops=flops, bytes_accessed=moved, transcendentals=0)


def pack_kernel(x_ref, out_ref):
    lane = lanes_of((8, 128))
    rows = [[x_ref[:, r, 128 * c : 128 * c + 128] for r in range(4)] for c in range(CHUNKS)]
    for c in range(CHUNKS):
        right, left = rows[(c + 1) % CHUNKS], rows[c - 1]
        for r in range(4):
            out_ref[c, 4 * r : 4 * r + 4, :] = rows[c][r]
        near, far = (
            jnp.where(lane < 64, jnp.concatenate([right[r], right[r + 2]], 0), jnp.concatenate([left[r], left[r + 2]], 0))
            for r in range(2)
        )
        far = jnp.where(lane < 64, pltpu.roll(far, 32, 1), pltpu.roll(far, 96, 1))
        out_ref[c, 16:24, :] = jnp.where((lane < 32) | (lane >= 96), near, far)


def unpacked(piece):
    lane, sub = lanes_of((8, 128)), lax.broadcasted_iota(jnp.int32, (8, 128), 0)
    first, second, near = piece[0:8], piece[8:16], piece[16:24]
    far = jnp.where(lane < 64, pltpu.roll(near, 96, 1), pltpu.roll(near, 32, 1))

    def joined(own, around):
        return jnp.where(sub < 4, own, around)

    def turned(x):
        return pltpu.roll(x, 4, 0)

    return (
        joined(first, turned(near)),
        joined(turned(first), turned(far)),
        joined(second, near),
        joined(turned(second), far),
    )


def pack(x):
    return pl.pallas_call(
        pack_kernel,
        out_shape=pltpu.VMEM((CHUNKS, 24, 128), jnp.float32),
        in_specs=whole(1),
        out_specs=whole(1)[0],
        cost_estimate=cost(100_000, 400_000),
        name="pack",
    )(x)


def folded(coeffs, sign):
    weights = [0.0] * PLANES
    for k, value in enumerate(coeffs, 1):
        weights[k % PLANES] += value
        weights[-k % PLANES] += sign * value
    return weights


def column_shifts(here, lane, reach):
    other = pltpu.roll(here, 4, 1)
    right = [pltpu.roll(jnp.where(lane < k, other, here), 128 - k, 2) for k in range(1, reach + 1)]
    left = [pltpu.roll(jnp.where(lane >= 128 - k, other, here), k, 2) for k in range(1, reach + 1)]
    return right, left


def plane_shifts(here, plane):
    over = jnp.where(plane < 3, pltpu.roll(here, 7, 1), pltpu.roll(here, 3, 1))
    under = jnp.where(plane > 0, pltpu.roll(here, 1, 1), pltpu.roll(here, 5, 1))
    return over, under


def plane_opposite(here, plane):
    return jnp.where(plane < 2, pltpu.roll(here, 6, 1), pltpu.roll(here, 2, 1))


def weighted(coeffs, terms):
    total = None
    for value, term in zip(coeffs, terms):
        total = value * term if total is None else total + value * term
    return total


def derivatives(load, low, lane, plane, second=True):
    here = load(low)
    right, left = column_shifts(here, lane, 4)
    up, down = ([load(low + s * k) for k in range(1, 5)] for s in (1, -1))
    over, under = plane_shifts(here, plane)
    _, forward, _, behind = folded(first_coeffs, -1.0)
    assert forward == -behind
    d_x = weighted(first_coeffs, [a - b for a, b in zip(up, down)])
    d_y = weighted(first_coeffs, [a - b for a, b in zip(right, left)])
    d_z = forward * (over - under)
    if not second:
        return d_x, d_y, d_z
    centre, near, far, _ = folded(second_coeffs, 1.0)
    lap = weighted(second_coeffs, [(a + b) + (c + d) for a, b, c, d in zip(up, down, right, left)])
    lap = lap + (3.0 * second_center + centre) * here
    lap = lap + (near * (over + under) + far * plane_opposite(here, plane))
    return d_x, d_y, d_z, lap


def flow_kernel(own_ref, low_ref, high_ref, out_ref, fields, middle, slopes, lifted):
    for ref, count, base in ((low_ref, 3, 0), (own_ref, 4, 12), (high_ref, 3, 28)):
        for j in range(count):
            for g in range(4):
                for r, row in enumerate(unpacked(ref[4 * j + g])):
                    fields[g, base + 4 * j + r] = row

    shape = (4, 8, 128)
    lane = lanes_of(shape)
    plane = lax.broadcasted_iota(jnp.int32, shape, 1) % 4

    def loader(ref, g):
        return lambda low: ref[g, pl.ds(low, 4)]

    def first(i, carry):
        low = 4 + 4 * i
        grads = derivatives(loader(fields, 3), low, lane, plane, second=False)
        u, v, w = (fields[f, pl.ds(low, 4)] for f in range(3))
        for g in range(3):
            d_x, d_y, d_z, lap = derivatives(loader(fields, g), low, lane, plane)
            slopes[g, pl.ds(4 * i, 4)] = grads[g]
            tend = viscosity * lap - (u * d_x + v * d_y + w * d_z) - grads[g]
            middle[g, pl.ds(4 * i, 4)] = (u, v, w)[g] + time_step * tend
        return carry

    lax.fori_loop(0, 8, first, 0)

    def second(i, carry):
        low = 4 + 4 * i
        u, v, w = (middle[f, pl.ds(low, 4)] for f in range(3))
        for g in range(3):
            d_x, d_y, d_z, lap = derivatives(loader(middle, g), low, lane, plane)
            tend = viscosity * lap - (u * d_x + v * d_y + w * d_z) - slopes[g, pl.ds(low, 4)]
            s = 0.5 * ((fields[g, pl.ds(low + 4, 4)] + (u, v, w)[g]) + time_step * tend)
            lifted[g, pl.ds(4 * i, 4)] = s
        return carry

    lax.fori_loop(0, 6, second, 0)

    lane, sub = lanes_of((8, 128)), lax.broadcasted_iota(jnp.int32, (8, 128), 0)
    odd_y, odd_z, first_row = lane % 2 == 1, sub % 2 == 1, sub < 4

    def chosen(odd, pair):
        return jnp.where(odd, jnp.float32(pair[1]), jnp.float32(pair[0]))

    taps = [chosen(odd_y, pair) for pair in filter_taps(None)]
    same, opposite = (chosen(odd_z, pair) for pair in filter_taps(PLANES))
    energy = [None] * 8
    for g in range(3):
        even = [lifted[g, 2 * i] for i in range(12)]
        odd = [lifted[g, 2 * i + 1] for i in range(12)]
        odd = [o + lift_alpha * (even[i] + even[i + 1]) for i, o in enumerate(odd[:11])]
        even = [None] + [even[i] + lift_beta * (odd[i] + odd[i - 1]) for i in range(1, 11)]
        odd = [None] + [odd[i] + lift_gamma * (even[i] + even[i + 1]) for i in range(1, 10)]
        even = [None, None] + [even[i] + lift_delta * (odd[i] + odd[i - 1]) for i in range(2, 10)]
        for pair in range(8):
            a, b = (even, odd)[pair // 4][2 + 2 * (pair % 4) : 4 + 2 * (pair % 4)]
            here = jnp.where(first_row, a, pltpu.roll(b, 4, 0))
            around = jnp.where(first_row, pltpu.roll(a, 4, 0), b)
            rows = taps[0] * here
            for k in range(1, 5):
                right = pltpu.roll(jnp.where(lane < k, around, here), 128 - k, 1)
                left = pltpu.roll(jnp.where(lane >= 128 - k, around, here), k, 1)
                rows = rows + taps[k] * (right + left)
            both = rows + jnp.where(sub % 4 < 2, pltpu.roll(rows, 6, 0), pltpu.roll(rows, 2, 0))
            others = jnp.where(odd_z, pltpu.roll(both, 1, 0), pltpu.roll(both, 7, 0))
            rows = rows + (same * both + opposite * others)
            scale = chosen(odd_z, (lift_scale, 1.0 / lift_scale)) * (lift_scale if pair < 4 else 1.0 / lift_scale)
            rows = rows * scale
            energy[pair] = rows * rows if g == 0 else energy[pair] + rows * rows
            for copy in range(4):
                out_ref[4 * copy + g, 8 * pair : 8 * pair + 8, :] = rows
    for pair in range(8):
        for copy in range(4):
            out_ref[4 * copy + 3, 8 * pair : 8 * pair + 8, :] = energy[pair]


def filter_taps(ring):
    size = ring or 32

    def lifted(s):
        for value, start in ((lift_alpha, 1), (lift_beta, 0), (lift_gamma, 1), (lift_delta, 0)):
            s = list(s)
            for i in range(start, size, 2):
                s[i] += value * (s[i - 1] + s[(i + 1) % size])
        return s

    answers = [lifted([1.0 if i == j else 0.0 for i in range(size)]) for j in range(size)]
    if ring:
        return tuple(tuple(answers[(i + d) % size][i] - (0.0 if d else 1.0) for i in (0, 1)) for d in (0, 1))
    scales = (lift_scale, 1.0 / lift_scale)
    return [tuple(answers[16 + odd + k][16 + odd] * scales[odd] for odd in (0, 1)) for k in range(5)]


def flow(own, low, high):
    return pl.pallas_call(
        flow_kernel,
        out_shape=pltpu.VMEM((16, 64, 128), jnp.float32),
        in_specs=whole(3),
        out_specs=whole(1)[0],
        scratch_shapes=[
            pltpu.VMEM((4, 40, 8, 128), jnp.float32),
            pltpu.VMEM((3, 32, 8, 128), jnp.float32),
            pltpu.VMEM((3, 32, 8, 128), jnp.float32),
            pltpu.VMEM((3, 24, 8, 128), jnp.float32),
        ],
        compiler_params=pltpu.CompilerParams(vmem_limit_bytes=VMEM_LIMIT),
        cost_estimate=cost(30_000_000, 1_000_000),
        name="flow",
    )(own, low, high)


def slots_kernel(owner_ref, owner_out, rank_out, rank_rows):
    bf16, f32 = jnp.bfloat16, jnp.float32
    row = lax.broadcasted_iota(jnp.int32, (128, 128), 0)
    lane = lanes_of((128, 128))
    before = jnp.concatenate([(row < lane).astype(f32), jnp.ones((128, 128), f32)], 1).astype(bf16)
    pencil = row
    base = jnp.zeros((128, 128), f32)
    for b in range(64):
        mine = owner_ref[b : b + 1, :] == pencil
        counts = jnp.dot(jnp.where(mine, 1.0, 0.0).astype(bf16), before, preferred_element_type=f32)
        ranks = jnp.where(mine, base + counts[:, 0:128], 0.0)
        rank_rows[b : b + 1, :] = jnp.sum(ranks, axis=0, keepdims=True)
        base = base + counts[:, 128:256]
    owners = owner_ref[...].astype(f32).astype(bf16)
    ranks = rank_rows[...].astype(bf16)
    for part in range(2):
        even = jnp.where(lane == 2 * (row - 64 * part), 1.0, 0.0).astype(bf16)
        odd = jnp.where(lane == 2 * (row - 64 * part) + 1, 1.0, 0.0).astype(bf16)
        for values, out in ((owners, owner_out), (ranks, rank_out)):
            from_even = jnp.dot(values, even, preferred_element_type=f32)
            from_odd = jnp.dot(values, odd, preferred_element_type=f32)
            for z in range(PLANES):
                plane = (0, 2, 1, 3)[z]
                low = from_even[16 * plane : 16 * plane + 8]
                high = from_odd[16 * plane + 8 : 16 * plane + 16]
                out[part, z, :, :] = (low + high).astype(jnp.int32)


def slots(owner_rows):
    shape = jax.ShapeDtypeStruct((2, PLANES, 8, 128), jnp.int32)
    return pl.pallas_call(
        slots_kernel,
        out_shape=(shape, shape),
        in_specs=whole(1),
        out_specs=tuple(whole(2)),
        scratch_shapes=[pltpu.VMEM((64, 128), jnp.float32)],
        compiler_params=pltpu.CompilerParams(vmem_limit_bytes=VMEM_LIMIT),
        cost_estimate=cost(600_000_000, 100_000),
        name="slots",
    )(owner_rows)


def gather_kernel(first_ref, table_ref, owner_ref, rank_ref, out_ref):
    bf16, f32 = jnp.bfloat16, jnp.float32
    first = first_ref[0]
    slot = lax.broadcasted_iota(jnp.int32, (256, 128), 0).astype(f32).astype(bf16)
    nothing = jnp.zeros((16, 128), bf16)

    def spread(row, rows):
        return jnp.broadcast_to(row, (rows, 128)).astype(f32).astype(bf16)

    def chunk(c, carry):
        moved = None
        for z in range(PLANES):
            values = table_ref[c, pl.ds(z, 16, stride=4), :]
            high = values.astype(bf16)
            low = (values - high.astype(f32)).astype(bf16)
            owner = owner_ref[c % 2, z, pl.ds(c // 2, 1), :]
            rank = rank_ref[c % 2, z, pl.ds(c // 2, 1), :]
            mine = owner % 4 == first
            pencil = owner // 4
            lower = spread(jnp.where(mine, pencil % 16, -1), 16)
            at = spread(jnp.where(mine, 128 * (pencil // 16) + rank, -1), 16)
            left = []
            for t in range(16):
                hit = lower == jnp.asarray(t, bf16)
                left.append(jnp.concatenate([jnp.where(hit, high, nothing), jnp.where(hit, low, nothing)], 1))
            ones = jnp.ones((16, 128), bf16)
            right = [jnp.where(at == slot[16 * k : 16 * k + 16], ones, nothing) for k in range(16)]
            right = jnp.concatenate(right, 0)
            part = lax.dot_general(
                jnp.concatenate(left, 0),
                jnp.concatenate([right, right], 1),
                (((1,), (1,)), ((), ())),
                preferred_element_type=f32,
            )
            moved = part if moved is None else moved + part
        for upper in range(2):
            part = moved[:, 128 * upper : 128 * upper + 128].reshape(16, 16, 128)
            rows = slice(16 * upper, 16 * upper + 16)
            out_ref[rows] = jnp.where(c == 0, part, out_ref[rows] + part)
        return carry

    lax.fori_loop(0, CHUNKS, chunk, 0, unroll=4)


def gather(first, table, owner, rank):
    return pl.pallas_call(
        gather_kernel,
        out_shape=jax.ShapeDtypeStruct((32, 16, 128), jnp.float32),
        in_specs=[pl.BlockSpec(memory_space=pltpu.SMEM)] + whole(3),
        out_specs=whole(1)[0],
        compiler_params=pltpu.CompilerParams(vmem_limit_bytes=VMEM_LIMIT),
        cost_estimate=cost(2_200_000_000, 1_000_000),
        name="gather",
    )(first, table, owner, rank)


def swap(x, axes):
    return lax.all_to_all(x, axes, split_axis=0, concat_axis=0, tiled=True)


def body(flow_state, line_owner):
    own = swap(pack(flow_state[0]), BLOCK_AXES)
    blocks = lax.axis_size(LONG_AXES)
    up = [(i, (i + 1) % blocks) for i in range(blocks)]
    own, lines = lax.optimization_barrier((own, line_owner.reshape(64, 128)))
    low = lax.ppermute(own[4:16], LONG_AXES, up)
    high = lax.ppermute(own[0:12], LONG_AXES, [(b, a) for a, b in up])
    owner, rank = slots(lines)
    first = lax.axis_index("y").astype(jnp.int32).reshape(1)
    own, owner, rank, first = lax.optimization_barrier((own, owner, rank, first))
    table = swap(flow(own, low, high), BLOCK_AXES)
    outgoing = gather(first, table, owner, rank)
    record = swap(outgoing, LONG_AXES)
    record = record.reshape(32, 2, 8, 128).transpose(1, 0, 2, 3).reshape(512, 128)
    return record[None, None]


def solution(mesh):
    split = Mesh(mesh.devices.reshape(2, 2, 2, 16, 4), ("xl", "co", "xh", "z", "y"))
    in_specs = (P(("xl", "co"), None, ("xh", "z", "y"), None), P())
    out_specs = P(("xl", "co"), ("xh", "z", "y"), None, None)
    return jax.shard_map(body, mesh=split, in_specs=in_specs, out_specs=out_specs, check_vma=False)
```

```python
import jax
import jax.numpy as jnp
from jax import lax
from jax.experimental import pallas as pl
from jax.experimental.pallas import tpu as pltpu
from jax.sharding import Mesh
from jax.sharding import PartitionSpec as P

BLOCK_AXES = ("y", "xl", "co")
LONG_AXES = ("xh", "z")
LAST_AXES = ("z", "xh")

time_step = 0.2
viscosity = 0.05
first_coeffs = (0.8, -0.2, 4.0 / 105.0, -1.0 / 280.0)
second_center = -205.0 / 72.0
second_coeffs = (1.6, -0.2, 8.0 / 315.0, -1.0 / 560.0)
lift_alpha = -1.586134342059924
lift_beta = -0.052980118572961
lift_gamma = 0.882911075530934
lift_delta = 0.443506852043971
lift_scale = 1.149604398860241

PLANES = 4
CHUNKS = 16
VMEM_LIMIT = 24 * 1024 * 1024


def lanes_of(shape):
    return lax.broadcasted_iota(jnp.int32, shape, len(shape) - 1)


def whole(count):
    return [pl.BlockSpec(memory_space=pltpu.VMEM)] * count


def cost(flops, moved):
    return pl.CostEstimate(flops=flops, bytes_accessed=moved, transcendentals=0)


def pack_kernel(x_ref, out_ref):
    lane = lanes_of((8, 128))
    rows = [[x_ref[:, r, 128 * c : 128 * c + 128] for r in range(4)] for c in range(CHUNKS)]
    for c in range(CHUNKS):
        right, left = rows[(c + 1) % CHUNKS], rows[c - 1]
        for r in range(4):
            out_ref[c, 4 * r : 4 * r + 4, :] = rows[c][r]
        near, far = (
            jnp.where(lane < 64, jnp.concatenate([right[r], right[r + 2]], 0), jnp.concatenate([left[r], left[r + 2]], 0))
            for r in range(2)
        )
        far = jnp.where(lane < 64, pltpu.roll(far, 32, 1), pltpu.roll(far, 96, 1))
        out_ref[c, 16:24, :] = jnp.where((lane < 32) | (lane >= 96), near, far)


def unpacked(piece):
    lane, sub = lanes_of((8, 128)), lax.broadcasted_iota(jnp.int32, (8, 128), 0)
    first, second, near = piece[0:8], piece[8:16], piece[16:24]
    far = jnp.where(lane < 64, pltpu.roll(near, 96, 1), pltpu.roll(near, 32, 1))

    def joined(own, around):
        return jnp.where(sub < 4, own, around)

    def turned(x):
        return pltpu.roll(x, 4, 0)

    return (
        joined(first, turned(near)),
        joined(turned(first), turned(far)),
        joined(second, near),
        joined(turned(second), far),
    )


def pack(x):
    return pl.pallas_call(
        pack_kernel,
        out_shape=pltpu.VMEM((CHUNKS, 24, 128), jnp.float32),
        in_specs=whole(1),
        out_specs=whole(1)[0],
        cost_estimate=cost(100_000, 400_000),
        name="pack",
    )(x)


def folded(coeffs, sign):
    weights = [0.0] * PLANES
    for k, value in enumerate(coeffs, 1):
        weights[k % PLANES] += value
        weights[-k % PLANES] += sign * value
    return weights


def column_shifts(here, lane, reach):
    other = pltpu.roll(here, 4, 1)
    right = [pltpu.roll(jnp.where(lane < k, other, here), 128 - k, 2) for k in range(1, reach + 1)]
    left = [pltpu.roll(jnp.where(lane >= 128 - k, other, here), k, 2) for k in range(1, reach + 1)]
    return right, left


def plane_shifts(here, plane):
    over = jnp.where(plane < 3, pltpu.roll(here, 7, 1), pltpu.roll(here, 3, 1))
    under = jnp.where(plane > 0, pltpu.roll(here, 1, 1), pltpu.roll(here, 5, 1))
    return over, under


def plane_opposite(here, plane):
    return jnp.where(plane < 2, pltpu.roll(here, 6, 1), pltpu.roll(here, 2, 1))


def weighted(coeffs, terms):
    total = None
    for value, term in zip(coeffs, terms):
        total = value * term if total is None else total + value * term
    return total


def derivatives(load, low, lane, plane, second=True):
    here = load(low)
    right, left = column_shifts(here, lane, 4)
    up, down = ([load(low + s * k) for k in range(1, 5)] for s in (1, -1))
    over, under = plane_shifts(here, plane)
    _, forward, _, behind = folded(first_coeffs, -1.0)
    assert forward == -behind
    d_x = weighted(first_coeffs, [a - b for a, b in zip(up, down)])
    d_y = weighted(first_coeffs, [a - b for a, b in zip(right, left)])
    d_z = forward * (over - under)
    if not second:
        return d_x, d_y, d_z
    centre, near, far, _ = folded(second_coeffs, 1.0)
    lap = weighted(second_coeffs, [(a + b) + (c + d) for a, b, c, d in zip(up, down, right, left)])
    lap = lap + (3.0 * second_center + centre) * here
    lap = lap + (near * (over + under) + far * plane_opposite(here, plane))
    return d_x, d_y, d_z, lap


def flow_kernel(own_ref, low_ref, high_ref, out_ref, fields, middle, slopes, lifted):
    for ref, count, base in ((low_ref, 3, 0), (own_ref, 4, 12), (high_ref, 3, 28)):
        for j in range(count):
            for g in range(4):
                for r, row in enumerate(unpacked(ref[4 * j + g])):
                    fields[g, base + 4 * j + r] = row

    shape = (4, 8, 128)
    lane = lanes_of(shape)
    plane = lax.broadcasted_iota(jnp.int32, shape, 1) % 4

    def loader(ref, g):
        return lambda low: ref[g, pl.ds(low, 4)]

    def first(i, carry):
        low = 4 + 4 * i
        grads = derivatives(loader(fields, 3), low, lane, plane, second=False)
        u, v, w = (fields[f, pl.ds(low, 4)] for f in range(3))
        for g in range(3):
            d_x, d_y, d_z, lap = derivatives(loader(fields, g), low, lane, plane)
            slopes[g, pl.ds(4 * i, 4)] = grads[g]
            tend = viscosity * lap - (u * d_x + v * d_y + w * d_z) - grads[g]
            middle[g, pl.ds(4 * i, 4)] = (u, v, w)[g] + time_step * tend
        return carry

    lax.fori_loop(0, 8, first, 0)

    def second(i, carry):
        low = 4 + 4 * i
        u, v, w = (middle[f, pl.ds(low, 4)] for f in range(3))
        for g in range(3):
            d_x, d_y, d_z, lap = derivatives(loader(middle, g), low, lane, plane)
            tend = viscosity * lap - (u * d_x + v * d_y + w * d_z) - slopes[g, pl.ds(low, 4)]
            s = 0.5 * ((fields[g, pl.ds(low + 4, 4)] + (u, v, w)[g]) + time_step * tend)
            lifted[g, pl.ds(4 * i, 4)] = s
        return carry

    lax.fori_loop(0, 6, second, 0)

    lane, sub = lanes_of((8, 128)), lax.broadcasted_iota(jnp.int32, (8, 128), 0)
    odd_y, odd_z, first_row = lane % 2 == 1, sub % 2 == 1, sub < 4

    def chosen(odd, pair):
        return jnp.where(odd, jnp.float32(pair[1]), jnp.float32(pair[0]))

    taps = [chosen(odd_y, pair) for pair in filter_taps(None)]
    same, opposite = (chosen(odd_z, pair) for pair in filter_taps(PLANES))
    energy = [None] * 8
    for g in range(3):
        even = [lifted[g, 2 * i] for i in range(12)]
        odd = [lifted[g, 2 * i + 1] for i in range(12)]
        odd = [o + lift_alpha * (even[i] + even[i + 1]) for i, o in enumerate(odd[:11])]
        even = [None] + [even[i] + lift_beta * (odd[i] + odd[i - 1]) for i in range(1, 11)]
        odd = [None] + [odd[i] + lift_gamma * (even[i] + even[i + 1]) for i in range(1, 10)]
        even = [None, None] + [even[i] + lift_delta * (odd[i] + odd[i - 1]) for i in range(2, 10)]
        for pair in range(8):
            a, b = (even, odd)[pair // 4][2 + 2 * (pair % 4) : 4 + 2 * (pair % 4)]
            here = jnp.where(first_row, a, pltpu.roll(b, 4, 0))
            around = jnp.where(first_row, pltpu.roll(a, 4, 0), b)
            rows = taps[0] * here
            for k in range(1, 5):
                right = pltpu.roll(jnp.where(lane < k, around, here), 128 - k, 1)
                left = pltpu.roll(jnp.where(lane >= 128 - k, around, here), k, 1)
                rows = rows + taps[k] * (right + left)
            both = rows + jnp.where(sub % 4 < 2, pltpu.roll(rows, 6, 0), pltpu.roll(rows, 2, 0))
            others = jnp.where(odd_z, pltpu.roll(both, 1, 0), pltpu.roll(both, 7, 0))
            rows = rows + (same * both + opposite * others)
            scale = chosen(odd_z, (lift_scale, 1.0 / lift_scale)) * (lift_scale if pair < 4 else 1.0 / lift_scale)
            rows = rows * scale
            energy[pair] = rows * rows if g == 0 else energy[pair] + rows * rows
            for copy in range(4):
                out_ref[4 * copy + g, 8 * pair : 8 * pair + 8, :] = rows
    for pair in range(8):
        for copy in range(4):
            out_ref[4 * copy + 3, 8 * pair : 8 * pair + 8, :] = energy[pair]


def filter_taps(ring):
    size = ring or 32

    def lifted(s):
        for value, start in ((lift_alpha, 1), (lift_beta, 0), (lift_gamma, 1), (lift_delta, 0)):
            s = list(s)
            for i in range(start, size, 2):
                s[i] += value * (s[i - 1] + s[(i + 1) % size])
        return s

    answers = [lifted([1.0 if i == j else 0.0 for i in range(size)]) for j in range(size)]
    if ring:
        return tuple(tuple(answers[(i + d) % size][i] - (0.0 if d else 1.0) for i in (0, 1)) for d in (0, 1))
    scales = (lift_scale, 1.0 / lift_scale)
    return [tuple(answers[16 + odd + k][16 + odd] * scales[odd] for odd in (0, 1)) for k in range(5)]


def flow(own, low, high):
    return pl.pallas_call(
        flow_kernel,
        out_shape=pltpu.VMEM((16, 64, 128), jnp.float32),
        in_specs=whole(3),
        out_specs=whole(1)[0],
        scratch_shapes=[
            pltpu.VMEM((4, 40, 8, 128), jnp.float32),
            pltpu.VMEM((3, 32, 8, 128), jnp.float32),
            pltpu.VMEM((3, 32, 8, 128), jnp.float32),
            pltpu.VMEM((3, 24, 8, 128), jnp.float32),
        ],
        compiler_params=pltpu.CompilerParams(vmem_limit_bytes=VMEM_LIMIT),
        cost_estimate=cost(30_000_000, 1_000_000),
        name="flow",
    )(own, low, high)


def slots_kernel(first_ref, owner_ref, lower_out, place_out, rank_rows):
    bf16, f32 = jnp.bfloat16, jnp.float32
    row = lax.broadcasted_iota(jnp.int32, (128, 128), 0)
    lane = lanes_of((128, 128))
    before = jnp.concatenate([(row < lane).astype(f32), jnp.ones((128, 128), f32)], 1).astype(bf16)
    pencil = row
    base = jnp.zeros((128, 128), f32)
    for b in range(64):
        mine = owner_ref[b : b + 1, :] == pencil
        counts = jnp.dot(jnp.where(mine, 1.0, 0.0).astype(bf16), before, preferred_element_type=f32)
        ranks = jnp.where(mine, base + counts[:, 0:128], 0.0)
        rank_rows[b : b + 1, :] = jnp.sum(ranks, axis=0, keepdims=True)
        base = base + counts[:, 128:256]
    owners, ranks = owner_ref[...].astype(f32), rank_rows[...]
    for part in range(2):
        even = jnp.where(lane == 2 * (row - 64 * part), 1.0, 0.0)
        odd = jnp.where(lane == 2 * (row - 64 * part) + 1, 1.0, 0.0)
        for z in range(PLANES):
            plane = (0, 2, 1, 3)[z]
            low, high = slice(16 * plane, 16 * plane + 8), slice(16 * plane + 8, 16 * plane + 16)
            owner, rank = (
                jnp.dot(values[low], even, preferred_element_type=f32)
                + jnp.dot(values[high], odd, preferred_element_type=f32)
                for values in (owners, ranks)
            )
            owner = owner.astype(jnp.int32)
            pencil = owner // 4
            lower = jnp.where(owner % 4 == first_ref[0], pencil % 16, -1)
            lower_out[part, z, :, :] = lower.astype(f32)
            place_out[part, z, :, :] = (128 * (pencil // 16)).astype(f32) + rank


def slots(first, owner_rows):
    shape = jax.ShapeDtypeStruct((2, PLANES, 8, 128), jnp.float32)
    return pl.pallas_call(
        slots_kernel,
        out_shape=(shape, shape),
        in_specs=[pl.BlockSpec(memory_space=pltpu.SMEM)] + whole(1),
        out_specs=tuple(whole(2)),
        scratch_shapes=[pltpu.VMEM((64, 128), jnp.float32)],
        compiler_params=pltpu.CompilerParams(vmem_limit_bytes=VMEM_LIMIT),
        cost_estimate=cost(600_000_000, 100_000),
        name="slots",
    )(first, owner_rows)


def gather_kernel(table_ref, lower_ref, place_ref, out_ref):
    bf16, f32 = jnp.bfloat16, jnp.float32
    slot = lax.broadcasted_iota(jnp.int32, (256, 128), 0).astype(f32).astype(bf16)
    nothing, ones = jnp.zeros((16, 128), bf16), jnp.ones((16, 128), bf16)
    total = None
    for c in range(CHUNKS):
        for pair in range(2):
            left, right = [], []
            for z in (2 * pair, 2 * pair + 1):
                values = table_ref[c, pl.ds(z, 16, stride=4), :]
                high = values.astype(bf16)
                low = (values - high.astype(f32)).astype(bf16)
                lower, place = (
                    jnp.broadcast_to(ref[c % 2, z, c // 2 : c // 2 + 1, :], (16, 128)).astype(bf16)
                    for ref in (lower_ref, place_ref)
                )
                hits = [lower == jnp.asarray(t, bf16) for t in range(16)]
                left.append(jnp.concatenate([jnp.where(hit, x, nothing) for x in (high, low) for hit in hits], 0))
                at = [jnp.where(place == slot[16 * k : 16 * k + 16], ones, nothing) for k in range(16)]
                right.append(jnp.concatenate(at, 0))
            part = lax.dot_general(
                jnp.concatenate(left, 1),
                jnp.concatenate(right, 1),
                (((1,), (1,)), ((), ())),
                preferred_element_type=f32,
            )
            total = part if total is None else total + part
    total = total[0:256] + total[256:512]
    for upper in range(2):
        out_ref[:, upper] = total[:, 128 * upper : 128 * upper + 128].reshape(16, 16, 128)


def gather(table, lower, place):
    return pl.pallas_call(
        gather_kernel,
        out_shape=jax.ShapeDtypeStruct((16, 2, 16, 128), jnp.float32),
        in_specs=whole(3),
        out_specs=whole(1)[0],
        compiler_params=pltpu.CompilerParams(vmem_limit_bytes=VMEM_LIMIT),
        cost_estimate=cost(2_200_000_000, 1_000_000),
        name="gather",
    )(table, lower, place)


def swap(x, axes):
    return lax.all_to_all(x, axes, split_axis=0, concat_axis=0, tiled=True)


def body(flow_state, line_owner):
    own = swap(pack(flow_state[0]), BLOCK_AXES)
    blocks = lax.axis_size(LONG_AXES)
    up = [(i, (i + 1) % blocks) for i in range(blocks)]
    own, lines = lax.optimization_barrier((own, line_owner.reshape(64, 128)))
    low = lax.ppermute(own[4:16], LONG_AXES, up)
    high = lax.ppermute(own[0:12], LONG_AXES, [(b, a) for a, b in up])
    first = lax.axis_index("y").astype(jnp.int32).reshape(1)
    own, lower, place = lax.optimization_barrier((own, *slots(first, lines)))
    table = swap(flow(own, low, high), BLOCK_AXES)
    outgoing = gather(table, lower, place).reshape(32, 16, 128)
    record = swap(outgoing, LAST_AXES)
    record = record.reshape(16, 2, 2, 8, 128).transpose(2, 1, 0, 3, 4).reshape(512, 128)
    return record[None, None]


def solution(mesh):
    split = Mesh(mesh.devices.reshape(2, 2, 2, 16, 4), ("xl", "co", "xh", "z", "y"))
    in_specs = (P(("xl", "co"), None, ("xh", "z", "y"), None), P())
    out_specs = P(("xl", "co"), ("xh", "z", "y"), None, None)
    return jax.shard_map(body, mesh=split, in_specs=in_specs, out_specs=out_specs, check_vma=False)
```

```python
import jax
import jax.numpy as jnp
import numpy as np
from jax import lax
from jax.experimental import pallas as pl
from jax.experimental.pallas import tpu as pltpu
from jax.sharding import Mesh
from jax.sharding import PartitionSpec as P

BLOCK_AXES = ("y", "xl", "co")
LONG_AXES = ("xh", "z")
LAST_AXES = ("z", "xh")

time_step = 0.2
viscosity = 0.05
first_coeffs = (0.8, -0.2, 4.0 / 105.0, -1.0 / 280.0)
second_center = -205.0 / 72.0
second_coeffs = (1.6, -0.2, 8.0 / 315.0, -1.0 / 560.0)
lift_alpha = -1.586134342059924
lift_beta = -0.052980118572961
lift_gamma = 0.882911075530934
lift_delta = 0.443506852043971
lift_scale = 1.149604398860241

PLANES = 4
CHUNKS = 16
VMEM_LIMIT = 24 * 1024 * 1024


def lanes_of(shape):
    return lax.broadcasted_iota(jnp.int32, shape, len(shape) - 1)


def whole(count):
    return [pl.BlockSpec(memory_space=pltpu.VMEM)] * count


def cost(flops, moved):
    return pl.CostEstimate(flops=flops, bytes_accessed=moved, transcendentals=0)


def pack_kernel(x_ref, out_ref):
    lane = lanes_of((8, 128))
    rows = [[x_ref[:, r, 128 * c : 128 * c + 128] for r in range(4)] for c in range(CHUNKS)]
    for c in range(CHUNKS):
        right, left = rows[(c + 1) % CHUNKS], rows[c - 1]
        for r in range(4):
            out_ref[c, 4 * r : 4 * r + 4, :] = rows[c][r]
        near, far = (
            jnp.where(lane < 64, jnp.concatenate([right[r], right[r + 2]], 0), jnp.concatenate([left[r], left[r + 2]], 0))
            for r in range(2)
        )
        far = jnp.where(lane < 64, pltpu.roll(far, 32, 1), pltpu.roll(far, 96, 1))
        out_ref[c, 16:24, :] = jnp.where((lane < 32) | (lane >= 96), near, far)


def unpacked(piece):
    lane, sub = lanes_of((8, 128)), lax.broadcasted_iota(jnp.int32, (8, 128), 0)
    first, second, near = piece[0:8], piece[8:16], piece[16:24]
    far = jnp.where(lane < 64, pltpu.roll(near, 96, 1), pltpu.roll(near, 32, 1))

    def joined(own, around):
        return jnp.where(sub < 4, own, around)

    def turned(x):
        return pltpu.roll(x, 4, 0)

    return (
        joined(first, turned(near)),
        joined(turned(first), turned(far)),
        joined(second, near),
        joined(turned(second), far),
    )


def pack(x):
    return pl.pallas_call(
        pack_kernel,
        out_shape=pltpu.VMEM((CHUNKS, 24, 128), jnp.float32),
        in_specs=whole(1),
        out_specs=whole(1)[0],
        cost_estimate=cost(100_000, 400_000),
        name="pack",
    )(x)


def folded(coeffs, sign):
    weights = [0.0] * PLANES
    for k, value in enumerate(coeffs, 1):
        weights[k % PLANES] += value
        weights[-k % PLANES] += sign * value
    return weights


def column_weights():
    apart = (np.arange(256)[:, None] - np.arange(128)[None, :]) % 256
    first, second = np.zeros((256, 128)), np.zeros((256, 128))
    taps = [np.resize(pair, 128) for pair in filter_taps(None)]
    lift = taps[0] * (apart == 0)
    for k in range(1, 5):
        lift += taps[k] * ((apart == k) | (apart == 256 - k))
        first += first_coeffs[k - 1] * ((apart == k) * 1.0 - (apart == 256 - k))
        second += second_coeffs[k - 1] * ((apart == k) * 1.0 + (apart == 256 - k))
    weights = np.concatenate([first, second, lift], 1)
    high = weights.astype(jnp.bfloat16)
    low = (weights - high.astype(np.float64)).astype(jnp.bfloat16)
    return np.concatenate([high, high, low], 0)


def weighted_lanes(rows, others, weights):
    both = jnp.concatenate([rows, others], 1)
    high = both.astype(jnp.bfloat16)
    low = (both - high.astype(jnp.float32)).astype(jnp.bfloat16)
    return jnp.dot(jnp.concatenate([high, low, high], 1), weights, preferred_element_type=jnp.float32)


def column_sums(values, weights_ref):
    rows = jnp.concatenate([v.reshape(32, 128) for v in values], 0)
    others = jnp.concatenate([pltpu.roll(v, 4, 1).reshape(32, 128) for v in values], 0)
    sums = weighted_lanes(rows, others, weights_ref[:, 0:256])
    return [
        tuple(sums[32 * n : 32 * n + 32, 128 * d : 128 * d + 128].reshape(4, 8, 128) for d in range(2))
        for n in range(len(values))
    ]


def plane_shifts(here, plane):
    over = jnp.where(plane < 3, pltpu.roll(here, 7, 1), pltpu.roll(here, 3, 1))
    under = jnp.where(plane > 0, pltpu.roll(here, 1, 1), pltpu.roll(here, 5, 1))
    return over, under


def plane_opposite(here, plane):
    return jnp.where(plane < 2, pltpu.roll(here, 6, 1), pltpu.roll(here, 2, 1))


def weighted(coeffs, terms):
    total = None
    for value, term in zip(coeffs, terms):
        total = value * term if total is None else total + value * term
    return total


def derivatives(load, low, along_y, plane, second=True):
    here = load(low)
    d_y, lap_y = along_y
    up, down = ([load(low + s * k) for k in range(1, 5)] for s in (1, -1))
    over, under = plane_shifts(here, plane)
    _, forward, _, behind = folded(first_coeffs, -1.0)
    assert forward == -behind
    d_x = weighted(first_coeffs, [a - b for a, b in zip(up, down)])
    d_z = forward * (over - under)
    if not second:
        return d_x, d_y, d_z
    centre, near, far, _ = folded(second_coeffs, 1.0)
    lap = weighted(second_coeffs, [a + b for a, b in zip(up, down)]) + lap_y
    lap = lap + (3.0 * second_center + centre) * here
    lap = lap + (near * (over + under) + far * plane_opposite(here, plane))
    return d_x, d_y, d_z, lap


def flow_kernel(weights_ref, own_ref, low_ref, high_ref, out_ref, fields, middle, slopes, lifted):
    for ref, count, base in ((low_ref, 3, 0), (own_ref, 4, 12), (high_ref, 3, 28)):
        for j in range(count):
            for g in range(4):
                for r, row in enumerate(unpacked(ref[4 * j + g])):
                    fields[g, base + 4 * j + r] = row

    plane = lax.broadcasted_iota(jnp.int32, (4, 8, 128), 1) % 4

    def loader(ref, g):
        return lambda low: ref[g, pl.ds(low, 4)]

    def first(i, carry):
        low = 4 + 4 * i
        along_y = column_sums([fields[f, pl.ds(low, 4)] for f in range(4)], weights_ref)
        grads = derivatives(loader(fields, 3), low, along_y[3], plane, second=False)
        u, v, w = (fields[f, pl.ds(low, 4)] for f in range(3))
        for g in range(3):
            d_x, d_y, d_z, lap = derivatives(loader(fields, g), low, along_y[g], plane)
            slopes[g, pl.ds(4 * i, 4)] = grads[g]
            tend = viscosity * lap - (u * d_x + v * d_y + w * d_z) - grads[g]
            middle[g, pl.ds(4 * i, 4)] = (u, v, w)[g] + time_step * tend
        return carry

    lax.fori_loop(0, 8, first, 0, unroll=4)

    def second(i, carry):
        low = 4 + 4 * i
        u, v, w = (middle[f, pl.ds(low, 4)] for f in range(3))
        along_y = column_sums([u, v, w], weights_ref)
        for g in range(3):
            d_x, d_y, d_z, lap = derivatives(loader(middle, g), low, along_y[g], plane)
            tend = viscosity * lap - (u * d_x + v * d_y + w * d_z) - slopes[g, pl.ds(low, 4)]
            s = 0.5 * ((fields[g, pl.ds(low + 4, 4)] + (u, v, w)[g]) + time_step * tend)
            lifted[g, pl.ds(4 * i, 4)] = s
        return carry

    lax.fori_loop(0, 6, second, 0, unroll=3)

    sub = lax.broadcasted_iota(jnp.int32, (8, 128), 0)
    odd_z, first_row = sub % 2 == 1, sub < 4

    def chosen(odd, pair):
        return jnp.where(odd, jnp.float32(pair[1]), jnp.float32(pair[0]))

    same, opposite = (chosen(odd_z, pair) for pair in filter_taps(PLANES))
    energy = [None] * 8
    for g in range(3):
        even = [lifted[g, 2 * i] for i in range(12)]
        odd = [lifted[g, 2 * i + 1] for i in range(12)]
        odd = [o + lift_alpha * (even[i] + even[i + 1]) for i, o in enumerate(odd[:11])]
        even = [None] + [even[i] + lift_beta * (odd[i] + odd[i - 1]) for i in range(1, 11)]
        odd = [None] + [odd[i] + lift_gamma * (even[i] + even[i + 1]) for i in range(1, 10)]
        even = [None, None] + [even[i] + lift_delta * (odd[i] + odd[i - 1]) for i in range(2, 10)]
        pairs = [(even, odd)[pair // 4][2 + 2 * (pair % 4) : 4 + 2 * (pair % 4)] for pair in range(8)]
        here = jnp.concatenate([jnp.where(first_row, a, pltpu.roll(b, 4, 0)) for a, b in pairs], 0)
        around = jnp.concatenate([jnp.where(first_row, pltpu.roll(a, 4, 0), b) for a, b in pairs], 0)
        along_y = weighted_lanes(here, around, weights_ref[:, 256:384])
        for pair in range(8):
            rows = along_y[8 * pair : 8 * pair + 8]
            both = rows + jnp.where(sub % 4 < 2, pltpu.roll(rows, 6, 0), pltpu.roll(rows, 2, 0))
            others = jnp.where(odd_z, pltpu.roll(both, 1, 0), pltpu.roll(both, 7, 0))
            rows = rows + (same * both + opposite * others)
            scale = chosen(odd_z, (lift_scale, 1.0 / lift_scale)) * (lift_scale if pair < 4 else 1.0 / lift_scale)
            rows = rows * scale
            energy[pair] = rows * rows if g == 0 else energy[pair] + rows * rows
            for copy in range(4):
                out_ref[4 * copy + g, 8 * pair : 8 * pair + 8, :] = rows
    for pair in range(8):
        for copy in range(4):
            out_ref[4 * copy + 3, 8 * pair : 8 * pair + 8, :] = energy[pair]


def filter_taps(ring):
    size = ring or 32

    def lifted(s):
        for value, start in ((lift_alpha, 1), (lift_beta, 0), (lift_gamma, 1), (lift_delta, 0)):
            s = list(s)
            for i in range(start, size, 2):
                s[i] += value * (s[i - 1] + s[(i + 1) % size])
        return s

    answers = [lifted([1.0 if i == j else 0.0 for i in range(size)]) for j in range(size)]
    if ring:
        return tuple(tuple(answers[(i + d) % size][i] - (0.0 if d else 1.0) for i in (0, 1)) for d in (0, 1))
    scales = (lift_scale, 1.0 / lift_scale)
    return [tuple(answers[16 + odd + k][16 + odd] * scales[odd] for odd in (0, 1)) for k in range(5)]


def flow(own, low, high):
    return pl.pallas_call(
        flow_kernel,
        out_shape=pltpu.VMEM((16, 64, 128), jnp.float32),
        in_specs=whole(4),
        out_specs=whole(1)[0],
        scratch_shapes=[
            pltpu.VMEM((4, 40, 8, 128), jnp.float32),
            pltpu.VMEM((3, 32, 8, 128), jnp.float32),
            pltpu.VMEM((3, 32, 8, 128), jnp.float32),
            pltpu.VMEM((3, 24, 8, 128), jnp.float32),
        ],
        compiler_params=pltpu.CompilerParams(vmem_limit_bytes=VMEM_LIMIT),
        cost_estimate=cost(30_000_000, 1_000_000),
        name="flow",
    )(jnp.asarray(column_weights()), own, low, high)


def slots_kernel(first_ref, owner_ref, lower_out, place_out, rank_rows):
    bf16, f32 = jnp.bfloat16, jnp.float32
    row = lax.broadcasted_iota(jnp.int32, (128, 128), 0)
    lane = lanes_of((128, 128))
    before = jnp.concatenate([(row < lane).astype(f32), jnp.ones((128, 128), f32)], 1).astype(bf16)
    pencil = row
    base = jnp.zeros((128, 128), f32)
    for b in range(64):
        mine = owner_ref[b : b + 1, :] == pencil
        counts = jnp.dot(jnp.where(mine, 1.0, 0.0).astype(bf16), before, preferred_element_type=f32)
        ranks = jnp.where(mine, base + counts[:, 0:128], 0.0)
        rank_rows[b : b + 1, :] = jnp.sum(ranks, axis=0, keepdims=True)
        base = base + counts[:, 128:256]
    owners, ranks = owner_ref[...].astype(f32), rank_rows[...]
    for part in range(2):
        even = jnp.where(lane == 2 * (row - 64 * part), 1.0, 0.0)
        odd = jnp.where(lane == 2 * (row - 64 * part) + 1, 1.0, 0.0)
        for z in range(PLANES):
            plane = (0, 2, 1, 3)[z]
            low, high = slice(16 * plane, 16 * plane + 8), slice(16 * plane + 8, 16 * plane + 16)
            owner, rank = (
                jnp.dot(values[low], even, preferred_element_type=f32)
                + jnp.dot(values[high], odd, preferred_element_type=f32)
                for values in (owners, ranks)
            )
            owner = owner.astype(jnp.int32)
            pencil = owner // 4
            lower = jnp.where(owner % 4 == first_ref[0], pencil % 16, -1)
            lower_out[part, z, :, :] = lower.astype(f32)
            place_out[part, z, :, :] = (128 * (pencil // 16)).astype(f32) + rank


def slots(first, owner_rows):
    shape = jax.ShapeDtypeStruct((2, PLANES, 8, 128), jnp.float32)
    return pl.pallas_call(
        slots_kernel,
        out_shape=(shape, shape),
        in_specs=[pl.BlockSpec(memory_space=pltpu.SMEM)] + whole(1),
        out_specs=tuple(whole(2)),
        scratch_shapes=[pltpu.VMEM((64, 128), jnp.float32)],
        compiler_params=pltpu.CompilerParams(vmem_limit_bytes=VMEM_LIMIT),
        cost_estimate=cost(600_000_000, 100_000),
        name="slots",
    )(first, owner_rows)


def gather_kernel(table_ref, lower_ref, place_ref, out_ref):
    bf16, f32 = jnp.bfloat16, jnp.float32
    slot = lax.broadcasted_iota(jnp.int32, (256, 128), 0).astype(f32).astype(bf16)
    nothing, ones = jnp.zeros((16, 128), bf16), jnp.ones((16, 128), bf16)
    total = None
    for c in range(CHUNKS):
        for pair in range(2):
            left, right = [], []
            for z in (2 * pair, 2 * pair + 1):
                values = table_ref[c, pl.ds(z, 16, stride=4), :]
                high = values.astype(bf16)
                low = (values - high.astype(f32)).astype(bf16)
                lower, place = (
                    jnp.broadcast_to(ref[c % 2, z, c // 2 : c // 2 + 1, :], (16, 128)).astype(bf16)
                    for ref in (lower_ref, place_ref)
                )
                hits = [lower == jnp.asarray(t, bf16) for t in range(16)]
                left.append(jnp.concatenate([jnp.where(hit, x, nothing) for x in (high, low) for hit in hits], 0))
                at = [jnp.where(place == slot[16 * k : 16 * k + 16], ones, nothing) for k in range(16)]
                right.append(jnp.concatenate(at, 0))
            part = lax.dot_general(
                jnp.concatenate(left, 1),
                jnp.concatenate(right, 1),
                (((1,), (1,)), ((), ())),
                preferred_element_type=f32,
            )
            total = part if total is None else total + part
    total = total[0:256] + total[256:512]
    for upper in range(2):
        out_ref[:, upper] = total[:, 128 * upper : 128 * upper + 128].reshape(16, 16, 128)


def gather(table, lower, place):
    return pl.pallas_call(
        gather_kernel,
        out_shape=jax.ShapeDtypeStruct((16, 2, 16, 128), jnp.float32),
        in_specs=whole(3),
        out_specs=whole(1)[0],
        compiler_params=pltpu.CompilerParams(vmem_limit_bytes=VMEM_LIMIT),
        cost_estimate=cost(2_200_000_000, 1_000_000),
        name="gather",
    )(table, lower, place)


def swap(x, axes):
    return lax.all_to_all(x, axes, split_axis=0, concat_axis=0, tiled=True)


def body(flow_state, line_owner):
    own = swap(pack(flow_state[0]), BLOCK_AXES)
    blocks = lax.axis_size(LONG_AXES)
    up = [(i, (i + 1) % blocks) for i in range(blocks)]
    own, lines = lax.optimization_barrier((own, line_owner.reshape(64, 128)))
    low = lax.ppermute(own[4:16], LONG_AXES, up)
    high = lax.ppermute(own[0:12], LONG_AXES, [(b, a) for a, b in up])
    first = lax.axis_index("y").astype(jnp.int32).reshape(1)
    own, lower, place = lax.optimization_barrier((own, *slots(first, lines)))
    table = swap(flow(own, low, high), BLOCK_AXES)
    outgoing = gather(table, lower, place).reshape(32, 16, 128)
    record = swap(outgoing, LAST_AXES)
    record = record.reshape(16, 2, 2, 8, 128).transpose(2, 1, 0, 3, 4).reshape(512, 128)
    return record[None, None]


def solution(mesh):
    split = Mesh(mesh.devices.reshape(2, 2, 2, 16, 4), ("xl", "co", "xh", "z", "y"))
    in_specs = (P(("xl", "co"), None, ("xh", "z", "y"), None), P())
    out_specs = P(("xl", "co"), ("xh", "z", "y"), None, None)
    return jax.shard_map(body, mesh=split, in_specs=in_specs, out_specs=out_specs, check_vma=False)
```

```python
import jax
import jax.numpy as jnp
import numpy as np
from jax import lax
from jax.experimental import pallas as pl
from jax.experimental.pallas import tpu as pltpu
from jax.sharding import Mesh
from jax.sharding import PartitionSpec as P

BLOCK_AXES = ("y", "xl", "co")
LONG_AXES = ("xh", "z")
LAST_AXES = ("z", "xh")

time_step = 0.2
viscosity = 0.05
first_coeffs = (0.8, -0.2, 4.0 / 105.0, -1.0 / 280.0)
second_center = -205.0 / 72.0
second_coeffs = (1.6, -0.2, 8.0 / 315.0, -1.0 / 560.0)
lift_alpha = -1.586134342059924
lift_beta = -0.052980118572961
lift_gamma = 0.882911075530934
lift_delta = 0.443506852043971
lift_scale = 1.149604398860241

PLANES = 4
CHUNKS = 16
SHIFT = 2
VMEM_LIMIT = 24 * 1024 * 1024


def lanes_of(shape):
    return lax.broadcasted_iota(jnp.int32, shape, len(shape) - 1)


def whole(count):
    return [pl.BlockSpec(memory_space=pltpu.VMEM)] * count


def cost(flops, moved):
    return pl.CostEstimate(flops=flops, bytes_accessed=moved, transcendentals=0)


def pack_kernel(x_ref, out_ref):
    lane = lanes_of((8, 128))
    rows = [[x_ref[:, r, 128 * c : 128 * c + 128] for r in range(4)] for c in range(CHUNKS)]
    for c in range(CHUNKS):
        right, left = rows[(c + 1) % CHUNKS], rows[c - 1]
        for r in range(4):
            out_ref[c, 4 * r : 4 * r + 4, :] = rows[c][r]
        near, far = (
            jnp.where(lane < 64, jnp.concatenate([right[r], right[r + 2]], 0), jnp.concatenate([left[r], left[r + 2]], 0))
            for r in range(2)
        )
        far = jnp.where(lane < 64, pltpu.roll(far, 32, 1), pltpu.roll(far, 96, 1))
        out_ref[c, 16:24, :] = jnp.where((lane < 32) | (lane >= 96), near, far)


def unpacked(piece):
    lane, sub = lanes_of((8, 128)), lax.broadcasted_iota(jnp.int32, (8, 128), 0)
    first, second, near = piece[0:8], piece[8:16], piece[16:24]
    far = jnp.where(lane < 64, pltpu.roll(near, 96, 1), pltpu.roll(near, 32, 1))

    def joined(own, around):
        return jnp.where(sub < 4, own, around)

    def turned(x):
        return pltpu.roll(x, 4, 0)

    return (
        joined(first, turned(near)),
        joined(turned(first), turned(far)),
        joined(second, near),
        joined(turned(second), far),
    )


def pack(x):
    return pl.pallas_call(
        pack_kernel,
        out_shape=pltpu.VMEM((CHUNKS, 24, 128), jnp.float32),
        in_specs=whole(1),
        out_specs=whole(1)[0],
        cost_estimate=cost(100_000, 400_000),
        name="pack",
    )(x)


def folded(coeffs, sign):
    weights = [0.0] * PLANES
    for k, value in enumerate(coeffs, 1):
        weights[k % PLANES] += value
        weights[-k % PLANES] += sign * value
    return weights


def column_weights():
    apart = (np.arange(256)[:, None] - np.arange(128)[None, :]) % 256
    first, second = np.zeros((256, 128)), np.zeros((256, 128))
    taps = [np.resize(pair, 128) for pair in filter_taps(None)]
    lift = taps[0] * (apart == 0)
    for k in range(1, 5):
        lift += taps[k] * ((apart == k) | (apart == 256 - k))
        first += first_coeffs[k - 1] * ((apart == k) * 1.0 - (apart == 256 - k))
        second += second_coeffs[k - 1] * ((apart == k) * 1.0 + (apart == 256 - k))
    weights = np.concatenate([first, second, lift], 1)
    high = weights.astype(jnp.bfloat16)
    low = (weights - high.astype(np.float64)).astype(jnp.bfloat16)
    return np.concatenate([high, high, low], 0)


def weighted_lanes(rows, others, weights):
    both = jnp.concatenate([rows, others], 1)
    high = both.astype(jnp.bfloat16)
    low = (both - high.astype(jnp.float32)).astype(jnp.bfloat16)
    return jnp.dot(jnp.concatenate([high, low, high], 1), weights, preferred_element_type=jnp.float32)


def column_sums(values, weights_ref):
    rows = jnp.concatenate([v.reshape(32, 128) for v in values], 0)
    others = jnp.concatenate([pltpu.roll(v, 4, 1).reshape(32, 128) for v in values], 0)
    sums = weighted_lanes(rows, others, weights_ref[:, 0:256])
    return [
        tuple(sums[32 * n : 32 * n + 32, 128 * d : 128 * d + 128].reshape(4, 8, 128) for d in range(2))
        for n in range(len(values))
    ]


def plane_shifts(here, plane):
    over = jnp.where(plane < 3, pltpu.roll(here, 7, 1), pltpu.roll(here, 3, 1))
    under = jnp.where(plane > 0, pltpu.roll(here, 1, 1), pltpu.roll(here, 5, 1))
    return over, under


def plane_opposite(here, plane):
    return jnp.where(plane < 2, pltpu.roll(here, 6, 1), pltpu.roll(here, 2, 1))


def weighted(coeffs, terms):
    total = None
    for value, term in zip(coeffs, terms):
        total = value * term if total is None else total + value * term
    return total


def derivatives(load, low, along_y, plane, second=True):
    here = load(low)
    d_y, lap_y = along_y
    up, down = ([load(low + s * k) for k in range(1, 5)] for s in (1, -1))
    over, under = plane_shifts(here, plane)
    _, forward, _, behind = folded(first_coeffs, -1.0)
    assert forward == -behind
    d_x = weighted(first_coeffs, [a - b for a, b in zip(up, down)])
    d_z = forward * (over - under)
    if not second:
        return d_x, d_y, d_z
    centre, near, far, _ = folded(second_coeffs, 1.0)
    lap = weighted(second_coeffs, [a + b for a, b in zip(up, down)]) + lap_y
    lap = lap + (3.0 * second_center + centre) * here
    lap = lap + (near * (over + under) + far * plane_opposite(here, plane))
    return d_x, d_y, d_z, lap


def flow_kernel(weights_ref, own_ref, low_ref, high_ref, out_ref, fields, middle, slopes, lifted):
    for ref, count, base in ((low_ref, 4, 0), (own_ref, 4, 16), (high_ref, 2, 32)):
        for j in range(count):
            for g in range(4):
                for r, row in enumerate(unpacked(ref[4 * j + g])):
                    fields[g, base + 4 * j + r] = row

    plane = lax.broadcasted_iota(jnp.int32, (4, 8, 128), 1) % 4

    def loader(ref, g):
        return lambda low: ref[g, pl.ds(low, 4)]

    def first(i, carry):
        low = 4 + 4 * i
        along_y = column_sums([fields[f, pl.ds(low, 4)] for f in range(4)], weights_ref)
        grads = derivatives(loader(fields, 3), low, along_y[3], plane, second=False)
        u, v, w = (fields[f, pl.ds(low, 4)] for f in range(3))
        for g in range(3):
            d_x, d_y, d_z, lap = derivatives(loader(fields, g), low, along_y[g], plane)
            slopes[g, pl.ds(4 * i, 4)] = grads[g]
            tend = viscosity * lap - (u * d_x + v * d_y + w * d_z) - grads[g]
            middle[g, pl.ds(4 * i, 4)] = (u, v, w)[g] + time_step * tend
        return carry

    lax.fori_loop(0, 8, first, 0, unroll=4)

    def second(i, carry):
        low = 4 + 4 * i
        u, v, w = (middle[f, pl.ds(low, 4)] for f in range(3))
        along_y = column_sums([u, v, w], weights_ref)
        for g in range(3):
            d_x, d_y, d_z, lap = derivatives(loader(middle, g), low, along_y[g], plane)
            tend = viscosity * lap - (u * d_x + v * d_y + w * d_z) - slopes[g, pl.ds(low, 4)]
            s = 0.5 * ((fields[g, pl.ds(low + 4, 4)] + (u, v, w)[g]) + time_step * tend)
            lifted[g, pl.ds(4 * i, 4)] = s
        return carry

    lax.fori_loop(0, 6, second, 0, unroll=3)

    sub = lax.broadcasted_iota(jnp.int32, (8, 128), 0)
    odd_z, first_row = sub % 2 == 1, sub < 4

    def chosen(odd, pair):
        return jnp.where(odd, jnp.float32(pair[1]), jnp.float32(pair[0]))

    same, opposite = (chosen(odd_z, pair) for pair in filter_taps(PLANES))
    energy = [None] * 8
    for g in range(3):
        even = [lifted[g, 2 * i] for i in range(12)]
        odd = [lifted[g, 2 * i + 1] for i in range(12)]
        odd = [o + lift_alpha * (even[i] + even[i + 1]) for i, o in enumerate(odd[:11])]
        even = [None] + [even[i] + lift_beta * (odd[i] + odd[i - 1]) for i in range(1, 11)]
        odd = [None] + [odd[i] + lift_gamma * (even[i] + even[i + 1]) for i in range(1, 10)]
        even = [None, None] + [even[i] + lift_delta * (odd[i] + odd[i - 1]) for i in range(2, 10)]
        pairs = [(even, odd)[pair // 4][2 + 2 * (pair % 4) : 4 + 2 * (pair % 4)] for pair in range(8)]
        here = jnp.concatenate([jnp.where(first_row, a, pltpu.roll(b, 4, 0)) for a, b in pairs], 0)
        around = jnp.concatenate([jnp.where(first_row, pltpu.roll(a, 4, 0), b) for a, b in pairs], 0)
        along_y = weighted_lanes(here, around, weights_ref[:, 256:384])
        for pair in range(8):
            rows = along_y[8 * pair : 8 * pair + 8]
            both = rows + jnp.where(sub % 4 < 2, pltpu.roll(rows, 6, 0), pltpu.roll(rows, 2, 0))
            others = jnp.where(odd_z, pltpu.roll(both, 1, 0), pltpu.roll(both, 7, 0))
            rows = rows + (same * both + opposite * others)
            scale = chosen(odd_z, (lift_scale, 1.0 / lift_scale)) * (lift_scale if pair < 4 else 1.0 / lift_scale)
            rows = rows * scale
            energy[pair] = rows * rows if g == 0 else energy[pair] + rows * rows
            for copy in range(4):
                out_ref[4 * copy + g, 8 * pair : 8 * pair + 8, :] = rows
    for pair in range(8):
        for copy in range(4):
            out_ref[4 * copy + 3, 8 * pair : 8 * pair + 8, :] = energy[pair]


def filter_taps(ring):
    size = ring or 32

    def lifted(s):
        for value, start in ((lift_alpha, 1), (lift_beta, 0), (lift_gamma, 1), (lift_delta, 0)):
            s = list(s)
            for i in range(start, size, 2):
                s[i] += value * (s[i - 1] + s[(i + 1) % size])
        return s

    answers = [lifted([1.0 if i == j else 0.0 for i in range(size)]) for j in range(size)]
    if ring:
        return tuple(tuple(answers[(i + d) % size][i] - (0.0 if d else 1.0) for i in (0, 1)) for d in (0, 1))
    scales = (lift_scale, 1.0 / lift_scale)
    return [tuple(answers[16 + odd + k][16 + odd] * scales[odd] for odd in (0, 1)) for k in range(5)]


def flow(own, low, high):
    return pl.pallas_call(
        flow_kernel,
        out_shape=pltpu.VMEM((16, 64, 128), jnp.float32),
        in_specs=whole(4),
        out_specs=whole(1)[0],
        scratch_shapes=[
            pltpu.VMEM((4, 40, 8, 128), jnp.float32),
            pltpu.VMEM((3, 32, 8, 128), jnp.float32),
            pltpu.VMEM((3, 32, 8, 128), jnp.float32),
            pltpu.VMEM((3, 24, 8, 128), jnp.float32),
        ],
        compiler_params=pltpu.CompilerParams(vmem_limit_bytes=VMEM_LIMIT),
        cost_estimate=cost(30_000_000, 1_000_000),
        name="flow",
    )(jnp.asarray(column_weights()), own, low, high)


def slots_kernel(first_ref, owner_ref, lower_out, place_out, rank_rows):
    bf16, f32 = jnp.bfloat16, jnp.float32
    row = lax.broadcasted_iota(jnp.int32, (128, 128), 0)
    lane = lanes_of((128, 128))
    before = jnp.concatenate([(row < lane).astype(f32), jnp.ones((128, 128), f32)], 1).astype(bf16)
    pencil = row
    base = jnp.zeros((128, 128), f32)
    for b in range(64):
        mine = owner_ref[b : b + 1, :] == pencil
        counts = jnp.dot(jnp.where(mine, 1.0, 0.0).astype(bf16), before, preferred_element_type=f32)
        ranks = jnp.where(mine, base + counts[:, 0:128], 0.0)
        rank_rows[b : b + 1, :] = jnp.sum(ranks, axis=0, keepdims=True)
        base = base + counts[:, 128:256]
    owners, ranks = owner_ref[...].astype(f32), rank_rows[...]
    for part in range(2):
        even = jnp.where(lane == 2 * (row - 64 * part), 1.0, 0.0)
        odd = jnp.where(lane == 2 * (row - 64 * part) + 1, 1.0, 0.0)
        for z in range(PLANES):
            plane = (0, 2, 1, 3)[z]
            low, high = slice(16 * plane, 16 * plane + 8), slice(16 * plane + 8, 16 * plane + 16)
            owner, rank = (
                jnp.dot(values[low], even, preferred_element_type=f32)
                + jnp.dot(values[high], odd, preferred_element_type=f32)
                for values in (owners, ranks)
            )
            owner = owner.astype(jnp.int32)
            pencil = owner // 4
            lower = jnp.where(owner % 4 == first_ref[0], pencil % 16, -1)
            lower_out[part, z, :, :] = lower.astype(f32)
            place_out[part, z, :, :] = (128 * (pencil // 16)).astype(f32) + rank


def slots(first, owner_rows):
    shape = jax.ShapeDtypeStruct((2, PLANES, 8, 128), jnp.float32)
    return pl.pallas_call(
        slots_kernel,
        out_shape=(shape, shape),
        in_specs=[pl.BlockSpec(memory_space=pltpu.SMEM)] + whole(1),
        out_specs=tuple(whole(2)),
        scratch_shapes=[pltpu.VMEM((64, 128), jnp.float32)],
        compiler_params=pltpu.CompilerParams(vmem_limit_bytes=VMEM_LIMIT),
        cost_estimate=cost(600_000_000, 100_000),
        name="slots",
    )(first, owner_rows)


def gather_kernel(table_ref, lower_ref, place_ref, out_ref):
    bf16, f32 = jnp.bfloat16, jnp.float32
    slot = lax.broadcasted_iota(jnp.int32, (256, 128), 0).astype(f32).astype(bf16)
    nothing, ones = jnp.zeros((16, 128), bf16), jnp.ones((16, 128), bf16)
    total = None
    for c in range(CHUNKS):
        for pair in range(2):
            left, right = [], []
            for z in (2 * pair, 2 * pair + 1):
                values = table_ref[c, pl.ds(z, 16, stride=4), :]
                high = values.astype(bf16)
                low = (values - high.astype(f32)).astype(bf16)
                lower, place = (
                    jnp.broadcast_to(ref[c % 2, z, c // 2 : c // 2 + 1, :], (16, 128)).astype(bf16)
                    for ref in (lower_ref, place_ref)
                )
                hits = [lower == jnp.asarray(t, bf16) for t in range(16)]
                left.append(jnp.concatenate([jnp.where(hit, x, nothing) for x in (high, low) for hit in hits], 0))
                at = [jnp.where(place == slot[16 * k : 16 * k + 16], ones, nothing) for k in range(16)]
                right.append(jnp.concatenate(at, 0))
            part = lax.dot_general(
                jnp.concatenate(left, 1),
                jnp.concatenate(right, 1),
                (((1,), (1,)), ((), ())),
                preferred_element_type=f32,
            )
            total = part if total is None else total + part
    total = total[0:256] + total[256:512]
    for upper in range(2):
        out_ref[:, upper] = total[:, 128 * upper : 128 * upper + 128].reshape(16, 16, 128)


def gather(table, lower, place):
    return pl.pallas_call(
        gather_kernel,
        out_shape=jax.ShapeDtypeStruct((16, 2, 16, 128), jnp.float32),
        in_specs=whole(3),
        out_specs=whole(1)[0],
        compiler_params=pltpu.CompilerParams(vmem_limit_bytes=VMEM_LIMIT),
        cost_estimate=cost(2_200_000_000, 1_000_000),
        name="gather",
    )(table, lower, place)


def swap(x, axes):
    return lax.all_to_all(x, axes, split_axis=0, concat_axis=0, tiled=True)


def body(flow_state, line_owner):
    own = swap(pack(flow_state[0]), BLOCK_AXES)
    blocks = lax.axis_size(LONG_AXES)
    up = [(i, (i + 1) % blocks) for i in range(blocks)]
    own, lines = lax.optimization_barrier((own, line_owner.reshape(64, 128)))
    low = lax.ppermute(own, LONG_AXES, up)
    high = lax.ppermute(own[0:8], LONG_AXES, [(b, a) for a, b in up])
    first = lax.axis_index("y").astype(jnp.int32).reshape(1)
    own, lower, place = lax.optimization_barrier((own, *slots(first, lines)))
    table = swap(flow(own, low, high), BLOCK_AXES)
    outgoing = gather(table, lower, place).reshape(32, 16, 128)
    record = swap(outgoing, LAST_AXES)
    record = record.reshape(16, 2, 2, 8, 128).transpose(2, 1, 0, 3, 4).reshape(2, 256, 128)
    record = jnp.roll(record, -SHIFT, 1).reshape(512, 128)
    return record[None, None]


def solution(mesh):
    split = Mesh(mesh.devices.reshape(2, 2, 2, 16, 4), ("xl", "co", "xh", "z", "y"))
    in_specs = (P(("xl", "co"), None, ("xh", "z", "y"), None), P())
    out_specs = P(("xl", "co"), ("xh", "z", "y"), None, None)
    return jax.shard_map(body, mesh=split, in_specs=in_specs, out_specs=out_specs, check_vma=False)
```

```python
import jax
import jax.numpy as jnp
import numpy as np
from jax import lax
from jax.experimental import pallas as pl
from jax.experimental.pallas import tpu as pltpu
from jax.sharding import Mesh
from jax.sharding import PartitionSpec as P

BLOCK_AXES = ("xl", "y", "co")
LONG_AXES = ("xh", "z")
LAST_AXES = ("z", "xh")

time_step = 0.2
viscosity = 0.05
first_coeffs = (0.8, -0.2, 4.0 / 105.0, -1.0 / 280.0)
second_center = -205.0 / 72.0
second_coeffs = (1.6, -0.2, 8.0 / 315.0, -1.0 / 560.0)
lift_alpha = -1.586134342059924
lift_beta = -0.052980118572961
lift_gamma = 0.882911075530934
lift_delta = 0.443506852043971
lift_scale = 1.149604398860241

PLANES = 4
CHUNKS = 16
SHIFT = 2
VMEM_LIMIT = 24 * 1024 * 1024


def lanes_of(shape):
    return lax.broadcasted_iota(jnp.int32, shape, len(shape) - 1)


def whole(count):
    return [pl.BlockSpec(memory_space=pltpu.VMEM)] * count


def cost(flops, moved):
    return pl.CostEstimate(flops=flops, bytes_accessed=moved, transcendentals=0)


def pack_kernel(x_ref, out_ref):
    lane = lanes_of((8, 128))
    rows = [[x_ref[:, r, 128 * c : 128 * c + 128] for r in range(4)] for c in range(CHUNKS)]
    for c in range(CHUNKS):
        right, left = rows[(c + 1) % CHUNKS], rows[c - 1]
        for r in range(4):
            out_ref[c, 4 * r : 4 * r + 4, :] = rows[c][r]
        near, far = (
            jnp.where(lane < 64, jnp.concatenate([right[r], right[r + 2]], 0), jnp.concatenate([left[r], left[r + 2]], 0))
            for r in range(2)
        )
        far = jnp.where(lane < 64, pltpu.roll(far, 32, 1), pltpu.roll(far, 96, 1))
        out_ref[c, 16:24, :] = jnp.where((lane < 32) | (lane >= 96), near, far)


def unpacked(piece):
    lane, sub = lanes_of((8, 128)), lax.broadcasted_iota(jnp.int32, (8, 128), 0)
    first, second, near = piece[0:8], piece[8:16], piece[16:24]
    far = jnp.where(lane < 64, pltpu.roll(near, 96, 1), pltpu.roll(near, 32, 1))

    def joined(own, around):
        return jnp.where(sub < 4, own, around)

    def turned(x):
        return pltpu.roll(x, 4, 0)

    return (
        joined(first, turned(near)),
        joined(turned(first), turned(far)),
        joined(second, near),
        joined(turned(second), far),
    )


def pack(x):
    return pl.pallas_call(
        pack_kernel,
        out_shape=pltpu.VMEM((CHUNKS, 24, 128), jnp.float32),
        in_specs=whole(1),
        out_specs=whole(1)[0],
        cost_estimate=cost(100_000, 400_000),
        name="pack",
    )(x)


def folded(coeffs, sign):
    weights = [0.0] * PLANES
    for k, value in enumerate(coeffs, 1):
        weights[k % PLANES] += value
        weights[-k % PLANES] += sign * value
    return weights


def column_weights():
    apart = (np.arange(256)[:, None] - np.arange(128)[None, :]) % 256
    first, second = np.zeros((256, 128)), np.zeros((256, 128))
    taps = [np.resize(pair, 128) for pair in filter_taps(None)]
    lift = taps[0] * (apart == 0)
    for k in range(1, 5):
        lift += taps[k] * ((apart == k) | (apart == 256 - k))
        first += first_coeffs[k - 1] * ((apart == k) * 1.0 - (apart == 256 - k))
        second += second_coeffs[k - 1] * ((apart == k) * 1.0 + (apart == 256 - k))
    weights = np.concatenate([first, second, lift], 1)
    high = weights.astype(jnp.bfloat16)
    low = (weights - high.astype(np.float64)).astype(jnp.bfloat16)
    return np.concatenate([high, high, low], 0)


def weighted_lanes(rows, others, weights):
    both = jnp.concatenate([rows, others], 1)
    high = both.astype(jnp.bfloat16)
    low = (both - high.astype(jnp.float32)).astype(jnp.bfloat16)
    return jnp.dot(jnp.concatenate([high, low, high], 1), weights, preferred_element_type=jnp.float32)


def column_sums(values, weights_ref):
    rows = jnp.concatenate([v.reshape(32, 128) for v in values], 0)
    others = jnp.concatenate([pltpu.roll(v, 4, 1).reshape(32, 128) for v in values], 0)
    sums = weighted_lanes(rows, others, weights_ref[:, 0:256])
    return [
        tuple(sums[32 * n : 32 * n + 32, 128 * d : 128 * d + 128].reshape(4, 8, 128) for d in range(2))
        for n in range(len(values))
    ]


def plane_shifts(here, plane):
    over = jnp.where(plane < 3, pltpu.roll(here, 7, 1), pltpu.roll(here, 3, 1))
    under = jnp.where(plane > 0, pltpu.roll(here, 1, 1), pltpu.roll(here, 5, 1))
    return over, under


def plane_opposite(here, plane):
    return jnp.where(plane < 2, pltpu.roll(here, 6, 1), pltpu.roll(here, 2, 1))


def weighted(coeffs, terms):
    total = None
    for value, term in zip(coeffs, terms):
        total = value * term if total is None else total + value * term
    return total


def derivatives(load, low, along_y, plane, second=True):
    here = load(low)
    d_y, lap_y = along_y
    up, down = ([load(low + s * k) for k in range(1, 5)] for s in (1, -1))
    over, under = plane_shifts(here, plane)
    _, forward, _, behind = folded(first_coeffs, -1.0)
    assert forward == -behind
    d_x = weighted(first_coeffs, [a - b for a, b in zip(up, down)])
    d_z = forward * (over - under)
    if not second:
        return d_x, d_y, d_z
    centre, near, far, _ = folded(second_coeffs, 1.0)
    lap = weighted(second_coeffs, [a + b for a, b in zip(up, down)]) + lap_y
    lap = lap + (3.0 * second_center + centre) * here
    lap = lap + (near * (over + under) + far * plane_opposite(here, plane))
    return d_x, d_y, d_z, lap


def place(g, j, count=4):
    sizes = {"xl": 2, "y": count, "co": 2}
    index = {"xl": g // 2, "y": j, "co": g % 2}
    at = 0
    for axis in BLOCK_AXES:
        at = at * sizes[axis] + index[axis]
    return at


def flow_kernel(weights_ref, own_ref, low_ref, high_ref, out_ref, fields, middle, slopes, lifted):
    for ref, count, base in ((low_ref, 4, 0), (own_ref, 4, 16), (high_ref, 2, 32)):
        for j in range(count):
            for g in range(4):
                for r, row in enumerate(unpacked(ref[place(g, j, count)])):
                    fields[g, base + 4 * j + r] = row

    plane = lax.broadcasted_iota(jnp.int32, (4, 8, 128), 1) % 4

    def loader(ref, g):
        return lambda low: ref[g, pl.ds(low, 4)]

    def first(i, carry):
        low = 4 + 4 * i
        along_y = column_sums([fields[f, pl.ds(low, 4)] for f in range(4)], weights_ref)
        grads = derivatives(loader(fields, 3), low, along_y[3], plane, second=False)
        u, v, w = (fields[f, pl.ds(low, 4)] for f in range(3))
        for g in range(3):
            d_x, d_y, d_z, lap = derivatives(loader(fields, g), low, along_y[g], plane)
            slopes[g, pl.ds(4 * i, 4)] = grads[g]
            tend = viscosity * lap - (u * d_x + v * d_y + w * d_z) - grads[g]
            middle[g, pl.ds(4 * i, 4)] = (u, v, w)[g] + time_step * tend
        return carry

    lax.fori_loop(0, 8, first, 0, unroll=4)

    def second(i, carry):
        low = 4 + 4 * i
        u, v, w = (middle[f, pl.ds(low, 4)] for f in range(3))
        along_y = column_sums([u, v, w], weights_ref)
        for g in range(3):
            d_x, d_y, d_z, lap = derivatives(loader(middle, g), low, along_y[g], plane)
            tend = viscosity * lap - (u * d_x + v * d_y + w * d_z) - slopes[g, pl.ds(low, 4)]
            s = 0.5 * ((fields[g, pl.ds(low + 4, 4)] + (u, v, w)[g]) + time_step * tend)
            lifted[g, pl.ds(4 * i, 4)] = s
        return carry

    lax.fori_loop(0, 6, second, 0, unroll=3)

    sub = lax.broadcasted_iota(jnp.int32, (8, 128), 0)
    odd_z, first_row = sub % 2 == 1, sub < 4

    def chosen(odd, pair):
        return jnp.where(odd, jnp.float32(pair[1]), jnp.float32(pair[0]))

    same, opposite = (chosen(odd_z, pair) for pair in filter_taps(PLANES))
    energy = [None] * 8
    for g in range(3):
        even = [lifted[g, 2 * i] for i in range(12)]
        odd = [lifted[g, 2 * i + 1] for i in range(12)]
        odd = [o + lift_alpha * (even[i] + even[i + 1]) for i, o in enumerate(odd[:11])]
        even = [None] + [even[i] + lift_beta * (odd[i] + odd[i - 1]) for i in range(1, 11)]
        odd = [None] + [odd[i] + lift_gamma * (even[i] + even[i + 1]) for i in range(1, 10)]
        even = [None, None] + [even[i] + lift_delta * (odd[i] + odd[i - 1]) for i in range(2, 10)]
        pairs = [(even, odd)[pair // 4][2 + 2 * (pair % 4) : 4 + 2 * (pair % 4)] for pair in range(8)]
        here = jnp.concatenate([jnp.where(first_row, a, pltpu.roll(b, 4, 0)) for a, b in pairs], 0)
        around = jnp.concatenate([jnp.where(first_row, pltpu.roll(a, 4, 0), b) for a, b in pairs], 0)
        along_y = weighted_lanes(here, around, weights_ref[:, 256:384])
        for pair in range(8):
            rows = along_y[8 * pair : 8 * pair + 8]
            both = rows + jnp.where(sub % 4 < 2, pltpu.roll(rows, 6, 0), pltpu.roll(rows, 2, 0))
            others = jnp.where(odd_z, pltpu.roll(both, 1, 0), pltpu.roll(both, 7, 0))
            rows = rows + (same * both + opposite * others)
            scale = chosen(odd_z, (lift_scale, 1.0 / lift_scale)) * (lift_scale if pair < 4 else 1.0 / lift_scale)
            rows = rows * scale
            energy[pair] = rows * rows if g == 0 else energy[pair] + rows * rows
            for copy in range(4):
                out_ref[place(g, copy), 8 * pair : 8 * pair + 8, :] = rows
    for pair in range(8):
        for copy in range(4):
            out_ref[place(3, copy), 8 * pair : 8 * pair + 8, :] = energy[pair]


def filter_taps(ring):
    size = ring or 32

    def lifted(s):
        for value, start in ((lift_alpha, 1), (lift_beta, 0), (lift_gamma, 1), (lift_delta, 0)):
            s = list(s)
            for i in range(start, size, 2):
                s[i] += value * (s[i - 1] + s[(i + 1) % size])
        return s

    answers = [lifted([1.0 if i == j else 0.0 for i in range(size)]) for j in range(size)]
    if ring:
        return tuple(tuple(answers[(i + d) % size][i] - (0.0 if d else 1.0) for i in (0, 1)) for d in (0, 1))
    scales = (lift_scale, 1.0 / lift_scale)
    return [tuple(answers[16 + odd + k][16 + odd] * scales[odd] for odd in (0, 1)) for k in range(5)]


def flow(own, low, high):
    return pl.pallas_call(
        flow_kernel,
        out_shape=pltpu.VMEM((16, 64, 128), jnp.float32),
        in_specs=whole(4),
        out_specs=whole(1)[0],
        scratch_shapes=[
            pltpu.VMEM((4, 40, 8, 128), jnp.float32),
            pltpu.VMEM((3, 32, 8, 128), jnp.float32),
            pltpu.VMEM((3, 32, 8, 128), jnp.float32),
            pltpu.VMEM((3, 24, 8, 128), jnp.float32),
        ],
        compiler_params=pltpu.CompilerParams(vmem_limit_bytes=VMEM_LIMIT),
        cost_estimate=cost(30_000_000, 1_000_000),
        name="flow",
    )(jnp.asarray(column_weights()), own, low, high)


def slots_kernel(first_ref, owner_ref, lower_out, place_out, rank_rows):
    bf16, f32 = jnp.bfloat16, jnp.float32
    row = lax.broadcasted_iota(jnp.int32, (128, 128), 0)
    lane = lanes_of((128, 128))
    before = jnp.concatenate([(row < lane).astype(f32), jnp.ones((128, 128), f32)], 1).astype(bf16)
    pencil = row
    base = jnp.zeros((128, 128), f32)
    for b in range(64):
        mine = owner_ref[b : b + 1, :] == pencil
        counts = jnp.dot(jnp.where(mine, 1.0, 0.0).astype(bf16), before, preferred_element_type=f32)
        ranks = jnp.where(mine, base + counts[:, 0:128], 0.0)
        rank_rows[b : b + 1, :] = jnp.sum(ranks, axis=0, keepdims=True)
        base = base + counts[:, 128:256]
    owners, ranks = owner_ref[...].astype(f32), rank_rows[...]
    for part in range(2):
        even = jnp.where(lane == 2 * (row - 64 * part), 1.0, 0.0)
        odd = jnp.where(lane == 2 * (row - 64 * part) + 1, 1.0, 0.0)
        for z in range(PLANES):
            plane = (0, 2, 1, 3)[z]
            low, high = slice(16 * plane, 16 * plane + 8), slice(16 * plane + 8, 16 * plane + 16)
            owner, rank = (
                jnp.dot(values[low], even, preferred_element_type=f32)
                + jnp.dot(values[high], odd, preferred_element_type=f32)
                for values in (owners, ranks)
            )
            owner = owner.astype(jnp.int32)
            pencil = owner // 4
            lower = jnp.where(owner % 4 == first_ref[0], pencil % 16, -1)
            lower_out[part, z, :, :] = lower.astype(f32)
            place_out[part, z, :, :] = (128 * (pencil // 16)).astype(f32) + rank


def slots(first, owner_rows):
    shape = jax.ShapeDtypeStruct((2, PLANES, 8, 128), jnp.float32)
    return pl.pallas_call(
        slots_kernel,
        out_shape=(shape, shape),
        in_specs=[pl.BlockSpec(memory_space=pltpu.SMEM)] + whole(1),
        out_specs=tuple(whole(2)),
        scratch_shapes=[pltpu.VMEM((64, 128), jnp.float32)],
        compiler_params=pltpu.CompilerParams(vmem_limit_bytes=VMEM_LIMIT),
        cost_estimate=cost(600_000_000, 100_000),
        name="slots",
    )(first, owner_rows)


def gather_kernel(table_ref, lower_ref, place_ref, out_ref):
    bf16, f32 = jnp.bfloat16, jnp.float32
    slot = lax.broadcasted_iota(jnp.int32, (256, 128), 0).astype(f32).astype(bf16)
    nothing, ones = jnp.zeros((16, 128), bf16), jnp.ones((16, 128), bf16)
    total = None
    for c in range(CHUNKS):
        for pair in range(2):
            left, right = [], []
            for z in (2 * pair, 2 * pair + 1):
                values = table_ref[c, pl.ds(z, 16, stride=4), :]
                high = values.astype(bf16)
                low = (values - high.astype(f32)).astype(bf16)
                lower, place = (
                    jnp.broadcast_to(ref[c % 2, z, c // 2 : c // 2 + 1, :], (16, 128)).astype(bf16)
                    for ref in (lower_ref, place_ref)
                )
                hits = [lower == jnp.asarray(t, bf16) for t in range(16)]
                left.append(jnp.concatenate([jnp.where(hit, x, nothing) for x in (high, low) for hit in hits], 0))
                at = [jnp.where(place == slot[16 * k : 16 * k + 16], ones, nothing) for k in range(16)]
                right.append(jnp.concatenate(at, 0))
            part = lax.dot_general(
                jnp.concatenate(left, 1),
                jnp.concatenate(right, 1),
                (((1,), (1,)), ((), ())),
                preferred_element_type=f32,
            )
            total = part if total is None else total + part
    total = total[0:256] + total[256:512]
    for upper in range(2):
        out_ref[:, upper] = total[:, 128 * upper : 128 * upper + 128].reshape(16, 16, 128)


def gather(table, lower, place):
    return pl.pallas_call(
        gather_kernel,
        out_shape=jax.ShapeDtypeStruct((16, 2, 16, 128), jnp.float32),
        in_specs=whole(3),
        out_specs=whole(1)[0],
        compiler_params=pltpu.CompilerParams(vmem_limit_bytes=VMEM_LIMIT),
        cost_estimate=cost(2_200_000_000, 1_000_000),
        name="gather",
    )(table, lower, place)


def swap(x, axes):
    return lax.all_to_all(x, axes, split_axis=0, concat_axis=0, tiled=True)


def body(flow_state, line_owner):
    own = swap(pack(flow_state[0]), BLOCK_AXES)
    blocks = lax.axis_size(LONG_AXES)
    up = [(i, (i + 1) % blocks) for i in range(blocks)]
    own, lines = lax.optimization_barrier((own, line_owner.reshape(64, 128)))
    low = lax.ppermute(own, LONG_AXES, up)
    high = lax.ppermute(own.reshape(2, 4, 2, 24, 128)[:, 0:2].reshape(8, 24, 128), LONG_AXES, [(b, a) for a, b in up])
    first = lax.axis_index("y").astype(jnp.int32).reshape(1)
    own, lower, place = lax.optimization_barrier((own, *slots(first, lines)))
    table = swap(flow(own, low, high), BLOCK_AXES)
    outgoing = gather(table, lower, place).reshape(32, 16, 128)
    record = swap(outgoing, LAST_AXES)
    record = record.reshape(16, 2, 2, 8, 128).transpose(2, 1, 0, 3, 4).reshape(2, 256, 128)
    record = jnp.roll(record, -SHIFT, 1).reshape(512, 128)
    return record[None, None]


def solution(mesh):
    split = Mesh(mesh.devices.reshape(2, 2, 2, 16, 4), ("xl", "co", "xh", "z", "y"))
    in_specs = (P(("xl", "co"), None, ("xh", "z", "y"), None), P())
    out_specs = P(("xl", "co"), ("xh", "z", "y"), None, None)
    return jax.shard_map(body, mesh=split, in_specs=in_specs, out_specs=out_specs, check_vma=False)
```

```python
import jax
import jax.numpy as jnp
import numpy as np
from jax import lax
from jax.experimental import pallas as pl
from jax.experimental.pallas import tpu as pltpu
from jax.sharding import Mesh
from jax.sharding import PartitionSpec as P

BLOCK_AXES = ("xl", "y", "co")
LONG_AXES = ("xh", "z")
LAST_AXES = ("z", "xh")

time_step = 0.2
viscosity = 0.05
first_coeffs = (0.8, -0.2, 4.0 / 105.0, -1.0 / 280.0)
second_center = -205.0 / 72.0
second_coeffs = (1.6, -0.2, 8.0 / 315.0, -1.0 / 560.0)
lift_alpha = -1.586134342059924
lift_beta = -0.052980118572961
lift_gamma = 0.882911075530934
lift_delta = 0.443506852043971
lift_scale = 1.149604398860241

PLANES = 4
CHUNKS = 16
SHIFT = 2
VMEM_LIMIT = 24 * 1024 * 1024


def lanes_of(shape):
    return lax.broadcasted_iota(jnp.int32, shape, len(shape) - 1)


def whole(count):
    return [pl.BlockSpec(memory_space=pltpu.VMEM)] * count


def cost(flops, moved):
    return pl.CostEstimate(flops=flops, bytes_accessed=moved, transcendentals=0)


def pack_kernel(x_ref, out_ref):
    lane = lanes_of((8, 128))
    rows = [[x_ref[:, r, 128 * c : 128 * c + 128] for r in range(4)] for c in range(CHUNKS)]
    for c in range(CHUNKS):
        right, left = rows[(c + 1) % CHUNKS], rows[c - 1]
        for r in range(4):
            out_ref[c, 4 * r : 4 * r + 4, :] = rows[c][r]
        near, far = (
            jnp.where(lane < 64, jnp.concatenate([right[r], right[r + 2]], 0), jnp.concatenate([left[r], left[r + 2]], 0))
            for r in range(2)
        )
        far = jnp.where(lane < 64, pltpu.roll(far, 32, 1), pltpu.roll(far, 96, 1))
        out_ref[c, 16:24, :] = jnp.where((lane < 32) | (lane >= 96), near, far)


def unpacked(piece):
    lane, sub = lanes_of((8, 128)), lax.broadcasted_iota(jnp.int32, (8, 128), 0)
    first, second, near = piece[0:8], piece[8:16], piece[16:24]
    far = jnp.where(lane < 64, pltpu.roll(near, 96, 1), pltpu.roll(near, 32, 1))

    def joined(own, around):
        return jnp.where(sub < 4, own, around)

    def turned(x):
        return pltpu.roll(x, 4, 0)

    return (
        joined(first, turned(near)),
        joined(turned(first), turned(far)),
        joined(second, near),
        joined(turned(second), far),
    )


def pack(x):
    return pl.pallas_call(
        pack_kernel,
        out_shape=pltpu.VMEM((CHUNKS, 24, 128), jnp.float32),
        in_specs=whole(1),
        out_specs=whole(1)[0],
        cost_estimate=cost(100_000, 400_000),
        name="pack",
    )(x)


def folded(coeffs, sign):
    weights = [0.0] * PLANES
    for k, value in enumerate(coeffs, 1):
        weights[k % PLANES] += value
        weights[-k % PLANES] += sign * value
    return weights


def column_weights():
    apart = (np.arange(256)[:, None] - np.arange(128)[None, :]) % 256
    first, second = np.zeros((256, 128)), np.zeros((256, 128))
    taps = [np.resize(pair, 128) for pair in filter_taps(None)]
    lift = taps[0] * (apart == 0)
    for k in range(1, 5):
        lift += taps[k] * ((apart == k) | (apart == 256 - k))
        first += first_coeffs[k - 1] * ((apart == k) * 1.0 - (apart == 256 - k))
        second += second_coeffs[k - 1] * ((apart == k) * 1.0 + (apart == 256 - k))
    weights = np.concatenate([first, second, lift], 1)
    high = weights.astype(jnp.bfloat16)
    low = (weights - high.astype(np.float64)).astype(jnp.bfloat16)
    return np.concatenate([high, high, low], 0)


def weighted_lanes(rows, others, weights):
    both = jnp.concatenate([rows, others], 1)
    high = both.astype(jnp.bfloat16)
    low = (both - high.astype(jnp.float32)).astype(jnp.bfloat16)
    return jnp.dot(jnp.concatenate([high, low, high], 1), weights, preferred_element_type=jnp.float32)


def column_sums(values, weights_ref):
    rows = jnp.concatenate([v.reshape(32, 128) for v in values], 0)
    others = jnp.concatenate([pltpu.roll(v, 4, 1).reshape(32, 128) for v in values], 0)
    sums = weighted_lanes(rows, others, weights_ref[:, 0:256])
    return [
        tuple(sums[32 * n : 32 * n + 32, 128 * d : 128 * d + 128].reshape(4, 8, 128) for d in range(2))
        for n in range(len(values))
    ]


def plane_shifts(here, plane):
    over = jnp.where(plane < 3, pltpu.roll(here, 7, 1), pltpu.roll(here, 3, 1))
    under = jnp.where(plane > 0, pltpu.roll(here, 1, 1), pltpu.roll(here, 5, 1))
    return over, under


def plane_opposite(here, plane):
    return jnp.where(plane < 2, pltpu.roll(here, 6, 1), pltpu.roll(here, 2, 1))


def weighted(coeffs, terms):
    total = None
    for value, term in zip(coeffs, terms):
        total = value * term if total is None else total + value * term
    return total


def derivatives(load, low, along_y, plane, second=True):
    here = load(low)
    d_y, lap_y = along_y
    up, down = ([load(low + s * k) for k in range(1, 5)] for s in (1, -1))
    over, under = plane_shifts(here, plane)
    _, forward, _, behind = folded(first_coeffs, -1.0)
    assert forward == -behind
    d_x = weighted(first_coeffs, [a - b for a, b in zip(up, down)])
    d_z = forward * (over - under)
    if not second:
        return d_x, d_y, d_z
    centre, near, far, _ = folded(second_coeffs, 1.0)
    lap = weighted(second_coeffs, [a + b for a, b in zip(up, down)]) + lap_y
    lap = lap + (3.0 * second_center + centre) * here
    lap = lap + (near * (over + under) + far * plane_opposite(here, plane))
    return d_x, d_y, d_z, lap


def place(g, j, count=4):
    sizes = {"xl": 2, "y": count, "co": 2}
    index = {"xl": g // 2, "y": j, "co": g % 2}
    at = 0
    for axis in BLOCK_AXES:
        at = at * sizes[axis] + index[axis]
    return at


def flow_kernel(weights_ref, own_ref, low_ref, high_ref, out_ref, fields, middle, slopes, lifted):
    for ref, count, base in ((low_ref, 4, 0), (own_ref, 4, 16), (high_ref, 2, 32)):
        for j in range(count):
            for g in range(4):
                for r, row in enumerate(unpacked(ref[place(g, j, count)])):
                    fields[g, base + 4 * j + r] = row

    plane = lax.broadcasted_iota(jnp.int32, (4, 8, 128), 1) % 4

    def loader(ref, g):
        return lambda low: ref[g, pl.ds(low, 4)]

    def first(i, carry):
        low = 4 + 4 * i
        along_y = column_sums([fields[f, pl.ds(low, 4)] for f in range(4)], weights_ref)
        grads = derivatives(loader(fields, 3), low, along_y[3], plane, second=False)
        u, v, w = (fields[f, pl.ds(low, 4)] for f in range(3))
        for g in range(3):
            d_x, d_y, d_z, lap = derivatives(loader(fields, g), low, along_y[g], plane)
            slopes[g, pl.ds(4 * i, 4)] = grads[g]
            tend = viscosity * lap - (u * d_x + v * d_y + w * d_z) - grads[g]
            middle[g, pl.ds(4 * i, 4)] = (u, v, w)[g] + time_step * tend
        return carry

    lax.fori_loop(0, 8, first, 0, unroll=8)

    def second(i, carry):
        low = 4 + 4 * i
        u, v, w = (middle[f, pl.ds(low, 4)] for f in range(3))
        along_y = column_sums([u, v, w], weights_ref)
        for g in range(3):
            d_x, d_y, d_z, lap = derivatives(loader(middle, g), low, along_y[g], plane)
            tend = viscosity * lap - (u * d_x + v * d_y + w * d_z) - slopes[g, pl.ds(low, 4)]
            s = 0.5 * ((fields[g, pl.ds(low + 4, 4)] + (u, v, w)[g]) + time_step * tend)
            lifted[g, pl.ds(4 * i, 4)] = s
        return carry

    lax.fori_loop(0, 6, second, 0, unroll=6)

    sub = lax.broadcasted_iota(jnp.int32, (8, 128), 0)
    odd_z, first_row = sub % 2 == 1, sub < 4

    def chosen(odd, pair):
        return jnp.where(odd, jnp.float32(pair[1]), jnp.float32(pair[0]))

    same, opposite = (chosen(odd_z, pair) for pair in filter_taps(PLANES))
    energy = [None] * 8
    for g in range(3):
        even = [lifted[g, 2 * i] for i in range(12)]
        odd = [lifted[g, 2 * i + 1] for i in range(12)]
        odd = [o + lift_alpha * (even[i] + even[i + 1]) for i, o in enumerate(odd[:11])]
        even = [None] + [even[i] + lift_beta * (odd[i] + odd[i - 1]) for i in range(1, 11)]
        odd = [None] + [odd[i] + lift_gamma * (even[i] + even[i + 1]) for i in range(1, 10)]
        even = [None, None] + [even[i] + lift_delta * (odd[i] + odd[i - 1]) for i in range(2, 10)]
        pairs = [(even, odd)[pair // 4][2 + 2 * (pair % 4) : 4 + 2 * (pair % 4)] for pair in range(8)]
        here = jnp.concatenate([jnp.where(first_row, a, pltpu.roll(b, 4, 0)) for a, b in pairs], 0)
        around = jnp.concatenate([jnp.where(first_row, pltpu.roll(a, 4, 0), b) for a, b in pairs], 0)
        along_y = weighted_lanes(here, around, weights_ref[:, 256:384])
        for pair in range(8):
            rows = along_y[8 * pair : 8 * pair + 8]
            both = rows + jnp.where(sub % 4 < 2, pltpu.roll(rows, 6, 0), pltpu.roll(rows, 2, 0))
            others = jnp.where(odd_z, pltpu.roll(both, 1, 0), pltpu.roll(both, 7, 0))
            rows = rows + (same * both + opposite * others)
            scale = chosen(odd_z, (lift_scale, 1.0 / lift_scale)) * (lift_scale if pair < 4 else 1.0 / lift_scale)
            rows = rows * scale
            energy[pair] = rows * rows if g == 0 else energy[pair] + rows * rows
            for copy in range(4):
                out_ref[place(g, copy), 8 * pair : 8 * pair + 8, :] = rows
    for pair in range(8):
        for copy in range(4):
            out_ref[place(3, copy), 8 * pair : 8 * pair + 8, :] = energy[pair]


def filter_taps(ring):
    size = ring or 32

    def lifted(s):
        for value, start in ((lift_alpha, 1), (lift_beta, 0), (lift_gamma, 1), (lift_delta, 0)):
            s = list(s)
            for i in range(start, size, 2):
                s[i] += value * (s[i - 1] + s[(i + 1) % size])
        return s

    answers = [lifted([1.0 if i == j else 0.0 for i in range(size)]) for j in range(size)]
    if ring:
        return tuple(tuple(answers[(i + d) % size][i] - (0.0 if d else 1.0) for i in (0, 1)) for d in (0, 1))
    scales = (lift_scale, 1.0 / lift_scale)
    return [tuple(answers[16 + odd + k][16 + odd] * scales[odd] for odd in (0, 1)) for k in range(5)]


def flow(own, low, high):
    return pl.pallas_call(
        flow_kernel,
        out_shape=pltpu.VMEM((16, 64, 128), jnp.float32),
        in_specs=whole(4),
        out_specs=whole(1)[0],
        scratch_shapes=[
            pltpu.VMEM((4, 40, 8, 128), jnp.float32),
            pltpu.VMEM((3, 32, 8, 128), jnp.float32),
            pltpu.VMEM((3, 32, 8, 128), jnp.float32),
            pltpu.VMEM((3, 24, 8, 128), jnp.float32),
        ],
        compiler_params=pltpu.CompilerParams(vmem_limit_bytes=VMEM_LIMIT),
        cost_estimate=cost(30_000_000, 1_000_000),
        name="flow",
    )(jnp.asarray(column_weights()), own, low, high)


def slots_kernel(first_ref, owner_ref, lower_out, place_out, rank_rows):
    bf16, f32 = jnp.bfloat16, jnp.float32
    row = lax.broadcasted_iota(jnp.int32, (128, 128), 0)
    lane = lanes_of((128, 128))
    before = jnp.concatenate([(row < lane).astype(f32), jnp.ones((128, 128), f32)], 1).astype(bf16)
    pencil = row
    base = jnp.zeros((128, 128), f32)
    for b in range(64):
        mine = owner_ref[b : b + 1, :] == pencil
        counts = jnp.dot(jnp.where(mine, 1.0, 0.0).astype(bf16), before, preferred_element_type=f32)
        ranks = jnp.where(mine, base + counts[:, 0:128], 0.0)
        rank_rows[b : b + 1, :] = jnp.sum(ranks, axis=0, keepdims=True)
        base = base + counts[:, 128:256]
    owners, ranks = owner_ref[...].astype(f32), rank_rows[...]
    for part in range(2):
        even = jnp.where(lane == 2 * (row - 64 * part), 1.0, 0.0)
        odd = jnp.where(lane == 2 * (row - 64 * part) + 1, 1.0, 0.0)
        for z in range(PLANES):
            plane = (0, 2, 1, 3)[z]
            low, high = slice(16 * plane, 16 * plane + 8), slice(16 * plane + 8, 16 * plane + 16)
            owner, rank = (
                jnp.dot(values[low], even, preferred_element_type=f32)
                + jnp.dot(values[high], odd, preferred_element_type=f32)
                for values in (owners, ranks)
            )
            owner = owner.astype(jnp.int32)
            pencil = owner // 4
            lower = jnp.where(owner % 4 == first_ref[0], pencil % 16, -1)
            lower_out[part, z, :, :] = lower.astype(f32)
            place_out[part, z, :, :] = (128 * (pencil // 16)).astype(f32) + rank


def slots(first, owner_rows):
    shape = jax.ShapeDtypeStruct((2, PLANES, 8, 128), jnp.float32)
    return pl.pallas_call(
        slots_kernel,
        out_shape=(shape, shape),
        in_specs=[pl.BlockSpec(memory_space=pltpu.SMEM)] + whole(1),
        out_specs=tuple(whole(2)),
        scratch_shapes=[pltpu.VMEM((64, 128), jnp.float32)],
        compiler_params=pltpu.CompilerParams(vmem_limit_bytes=VMEM_LIMIT),
        cost_estimate=cost(600_000_000, 100_000),
        name="slots",
    )(first, owner_rows)


def gather_kernel(table_ref, lower_ref, place_ref, out_ref):
    bf16, f32 = jnp.bfloat16, jnp.float32
    slot = lax.broadcasted_iota(jnp.int32, (256, 128), 0).astype(f32).astype(bf16)
    nothing, ones = jnp.zeros((16, 128), bf16), jnp.ones((16, 128), bf16)
    total = None
    for c in range(CHUNKS):
        for pair in range(2):
            left, right = [], []
            for z in (2 * pair, 2 * pair + 1):
                values = table_ref[c, pl.ds(z, 16, stride=4), :]
                high = values.astype(bf16)
                low = (values - high.astype(f32)).astype(bf16)
                lower, place = (
                    jnp.broadcast_to(ref[c % 2, z, c // 2 : c // 2 + 1, :], (16, 128)).astype(bf16)
                    for ref in (lower_ref, place_ref)
                )
                hits = [lower == jnp.asarray(t, bf16) for t in range(16)]
                left.append(jnp.concatenate([jnp.where(hit, x, nothing) for x in (high, low) for hit in hits], 0))
                at = [jnp.where(place == slot[16 * k : 16 * k + 16], ones, nothing) for k in range(16)]
                right.append(jnp.concatenate(at, 0))
            part = lax.dot_general(
                jnp.concatenate(left, 1),
                jnp.concatenate(right, 1),
                (((1,), (1,)), ((), ())),
                preferred_element_type=f32,
            )
            total = part if total is None else total + part
    total = total[0:256] + total[256:512]
    for upper in range(2):
        out_ref[:, upper] = total[:, 128 * upper : 128 * upper + 128].reshape(16, 16, 128)


def gather(table, lower, place):
    return pl.pallas_call(
        gather_kernel,
        out_shape=jax.ShapeDtypeStruct((16, 2, 16, 128), jnp.float32),
        in_specs=whole(3),
        out_specs=whole(1)[0],
        compiler_params=pltpu.CompilerParams(vmem_limit_bytes=VMEM_LIMIT),
        cost_estimate=cost(2_200_000_000, 1_000_000),
        name="gather",
    )(table, lower, place)


def swap(x, axes):
    return lax.all_to_all(x, axes, split_axis=0, concat_axis=0, tiled=True)


def body(flow_state, line_owner):
    own = swap(pack(flow_state[0]), BLOCK_AXES)
    blocks = lax.axis_size(LONG_AXES)
    up = [(i, (i + 1) % blocks) for i in range(blocks)]
    own, lines = lax.optimization_barrier((own, line_owner.reshape(64, 128)))
    low = lax.ppermute(own, LONG_AXES, up)
    high = lax.ppermute(own.reshape(2, 4, 2, 24, 128)[:, 0:2].reshape(8, 24, 128), LONG_AXES, [(b, a) for a, b in up])
    first = lax.axis_index("y").astype(jnp.int32).reshape(1)
    own, lower, place = lax.optimization_barrier((own, *slots(first, lines)))
    table = swap(flow(own, low, high), BLOCK_AXES)
    outgoing = gather(table, lower, place).reshape(32, 16, 128)
    record = swap(outgoing, LAST_AXES)
    record = record.reshape(16, 2, 2, 8, 128).transpose(2, 1, 0, 3, 4).reshape(2, 256, 128)
    record = jnp.roll(record, -SHIFT, 1).reshape(512, 128)
    return record[None, None]


def solution(mesh):
    split = Mesh(mesh.devices.reshape(2, 2, 2, 16, 4), ("xl", "co", "xh", "z", "y"))
    in_specs = (P(("xl", "co"), None, ("xh", "z", "y"), None), P())
    out_specs = P(("xl", "co"), ("xh", "z", "y"), None, None)
    return jax.shard_map(body, mesh=split, in_specs=in_specs, out_specs=out_specs, check_vma=False)
```

```python
import jax
import jax.numpy as jnp
import numpy as np
from jax import lax
from jax.experimental import pallas as pl
from jax.experimental.pallas import tpu as pltpu
from jax.sharding import Mesh
from jax.sharding import PartitionSpec as P

BLOCK_AXES = ("xl", "y", "co")
LONG_AXES = ("xh", "z")
LAST_AXES = ("z", "xh")

time_step = 0.2
viscosity = 0.05
first_coeffs = (0.8, -0.2, 4.0 / 105.0, -1.0 / 280.0)
second_center = -205.0 / 72.0
second_coeffs = (1.6, -0.2, 8.0 / 315.0, -1.0 / 560.0)
lift_alpha = -1.586134342059924
lift_beta = -0.052980118572961
lift_gamma = 0.882911075530934
lift_delta = 0.443506852043971
lift_scale = 1.149604398860241

PLANES = 4
CHUNKS = 16
SHIFT = 2
VMEM_LIMIT = 24 * 1024 * 1024


def lanes_of(shape):
    return lax.broadcasted_iota(jnp.int32, shape, len(shape) - 1)


def whole(count):
    return [pl.BlockSpec(memory_space=pltpu.VMEM)] * count


def cost(flops, moved):
    return pl.CostEstimate(flops=flops, bytes_accessed=moved, transcendentals=0)


def pack_kernel(far_ref, out_ref, x_ref, arrived):
    copies = [pltpu.make_async_copy(far_ref.at[z], x_ref.at[z], arrived.at[z]) for z in range(PLANES)]
    for copy in copies:
        copy.start()
    for copy in copies:
        copy.wait()
    lane = lanes_of((8, 128))
    rows = [[x_ref[:, r, 128 * c : 128 * c + 128] for r in range(4)] for c in range(CHUNKS)]
    for c in range(CHUNKS):
        right, left = rows[(c + 1) % CHUNKS], rows[c - 1]
        for r in range(4):
            out_ref[c, 4 * r : 4 * r + 4, :] = rows[c][r]
        near, far = (
            jnp.where(lane < 64, jnp.concatenate([right[r], right[r + 2]], 0), jnp.concatenate([left[r], left[r + 2]], 0))
            for r in range(2)
        )
        far = jnp.where(lane < 64, pltpu.roll(far, 32, 1), pltpu.roll(far, 96, 1))
        out_ref[c, 16:24, :] = jnp.where((lane < 32) | (lane >= 96), near, far)


def unpacked(piece):
    lane, sub = lanes_of((8, 128)), lax.broadcasted_iota(jnp.int32, (8, 128), 0)
    first, second, near = piece[0:8], piece[8:16], piece[16:24]
    far = jnp.where(lane < 64, pltpu.roll(near, 96, 1), pltpu.roll(near, 32, 1))

    def joined(own, around):
        return jnp.where(sub < 4, own, around)

    def turned(x):
        return pltpu.roll(x, 4, 0)

    return (
        joined(first, turned(near)),
        joined(turned(first), turned(far)),
        joined(second, near),
        joined(turned(second), far),
    )


def pack(x):
    return pl.pallas_call(
        pack_kernel,
        out_shape=pltpu.VMEM((CHUNKS, 24, 128), jnp.float32),
        in_specs=[pl.BlockSpec(memory_space=pl.ANY)],
        out_specs=whole(1)[0],
        scratch_shapes=[pltpu.VMEM((PLANES, 4, 2048), jnp.float32), pltpu.SemaphoreType.DMA((PLANES,))],
        cost_estimate=cost(100_000, 400_000),
        name="pack",
    )(x)


def folded(coeffs, sign):
    weights = [0.0] * PLANES
    for k, value in enumerate(coeffs, 1):
        weights[k % PLANES] += value
        weights[-k % PLANES] += sign * value
    return weights


def column_weights():
    apart = (np.arange(256)[:, None] - np.arange(128)[None, :]) % 256
    first, second = np.zeros((256, 128)), np.zeros((256, 128))
    taps = [np.resize(pair, 128) for pair in filter_taps(None)]
    lift = taps[0] * (apart == 0)
    for k in range(1, 5):
        lift += taps[k] * ((apart == k) | (apart == 256 - k))
        first += first_coeffs[k - 1] * ((apart == k) * 1.0 - (apart == 256 - k))
        second += second_coeffs[k - 1] * ((apart == k) * 1.0 + (apart == 256 - k))
    weights = np.concatenate([first, second, lift], 1)
    high = weights.astype(jnp.bfloat16)
    low = (weights - high.astype(np.float64)).astype(jnp.bfloat16)
    return np.concatenate([high, high, low], 0)


def weighted_lanes(rows, others, weights):
    both = jnp.concatenate([rows, others], 1)
    high = both.astype(jnp.bfloat16)
    low = (both - high.astype(jnp.float32)).astype(jnp.bfloat16)
    return jnp.dot(jnp.concatenate([high, low, high], 1), weights, preferred_element_type=jnp.float32)


def column_sums(values, weights_ref):
    rows = jnp.concatenate([v.reshape(32, 128) for v in values], 0)
    others = jnp.concatenate([pltpu.roll(v, 4, 1).reshape(32, 128) for v in values], 0)
    sums = weighted_lanes(rows, others, weights_ref[:, 0:256])
    return [
        tuple(sums[32 * n : 32 * n + 32, 128 * d : 128 * d + 128].reshape(4, 8, 128) for d in range(2))
        for n in range(len(values))
    ]


def plane_shifts(here, plane):
    over = jnp.where(plane < 3, pltpu.roll(here, 7, 1), pltpu.roll(here, 3, 1))
    under = jnp.where(plane > 0, pltpu.roll(here, 1, 1), pltpu.roll(here, 5, 1))
    return over, under


def plane_opposite(here, plane):
    return jnp.where(plane < 2, pltpu.roll(here, 6, 1), pltpu.roll(here, 2, 1))


def weighted(coeffs, terms):
    total = None
    for value, term in zip(coeffs, terms):
        total = value * term if total is None else total + value * term
    return total


def derivatives(load, low, along_y, plane, second=True):
    here = load(low)
    d_y, lap_y = along_y
    up, down = ([load(low + s * k) for k in range(1, 5)] for s in (1, -1))
    over, under = plane_shifts(here, plane)
    _, forward, _, behind = folded(first_coeffs, -1.0)
    assert forward == -behind
    d_x = weighted(first_coeffs, [a - b for a, b in zip(up, down)])
    d_z = forward * (over - under)
    if not second:
        return d_x, d_y, d_z
    centre, near, far, _ = folded(second_coeffs, 1.0)
    lap = weighted(second_coeffs, [a + b for a, b in zip(up, down)]) + lap_y
    lap = lap + (3.0 * second_center + centre) * here
    lap = lap + (near * (over + under) + far * plane_opposite(here, plane))
    return d_x, d_y, d_z, lap


def place(g, j, count=4):
    sizes = {"xl": 2, "y": count, "co": 2}
    index = {"xl": g // 2, "y": j, "co": g % 2}
    at = 0
    for axis in BLOCK_AXES:
        at = at * sizes[axis] + index[axis]
    return at


def flow_kernel(weights_ref, own_ref, low_ref, high_ref, out_ref, fields, middle, slopes, lifted):
    for ref, count, base in ((low_ref, 4, 0), (own_ref, 4, 16), (high_ref, 2, 32)):
        for j in range(count):
            for g in range(4):
                for r, row in enumerate(unpacked(ref[place(g, j, count)])):
                    fields[g, base + 4 * j + r] = row

    plane = lax.broadcasted_iota(jnp.int32, (4, 8, 128), 1) % 4

    def loader(ref, g):
        return lambda low: ref[g, pl.ds(low, 4)]

    def first(i, carry):
        low = 4 + 4 * i
        along_y = column_sums([fields[f, pl.ds(low, 4)] for f in range(4)], weights_ref)
        grads = derivatives(loader(fields, 3), low, along_y[3], plane, second=False)
        u, v, w = (fields[f, pl.ds(low, 4)] for f in range(3))
        for g in range(3):
            d_x, d_y, d_z, lap = derivatives(loader(fields, g), low, along_y[g], plane)
            slopes[g, pl.ds(4 * i, 4)] = grads[g]
            tend = viscosity * lap - (u * d_x + v * d_y + w * d_z) - grads[g]
            middle[g, pl.ds(4 * i, 4)] = (u, v, w)[g] + time_step * tend
        return carry

    lax.fori_loop(0, 8, first, 0, unroll=8)

    def second(i, carry):
        low = 4 + 4 * i
        u, v, w = (middle[f, pl.ds(low, 4)] for f in range(3))
        along_y = column_sums([u, v, w], weights_ref)
        for g in range(3):
            d_x, d_y, d_z, lap = derivatives(loader(middle, g), low, along_y[g], plane)
            tend = viscosity * lap - (u * d_x + v * d_y + w * d_z) - slopes[g, pl.ds(low, 4)]
            s = 0.5 * ((fields[g, pl.ds(low + 4, 4)] + (u, v, w)[g]) + time_step * tend)
            lifted[g, pl.ds(4 * i, 4)] = s
        return carry

    lax.fori_loop(0, 6, second, 0, unroll=6)

    sub = lax.broadcasted_iota(jnp.int32, (8, 128), 0)
    odd_z, first_row = sub % 2 == 1, sub < 4

    def chosen(odd, pair):
        return jnp.where(odd, jnp.float32(pair[1]), jnp.float32(pair[0]))

    same, opposite = (chosen(odd_z, pair) for pair in filter_taps(PLANES))
    energy = [None] * 8
    for g in range(3):
        even = [lifted[g, 2 * i] for i in range(12)]
        odd = [lifted[g, 2 * i + 1] for i in range(12)]
        odd = [o + lift_alpha * (even[i] + even[i + 1]) for i, o in enumerate(odd[:11])]
        even = [None] + [even[i] + lift_beta * (odd[i] + odd[i - 1]) for i in range(1, 11)]
        odd = [None] + [odd[i] + lift_gamma * (even[i] + even[i + 1]) for i in range(1, 10)]
        even = [None, None] + [even[i] + lift_delta * (odd[i] + odd[i - 1]) for i in range(2, 10)]
        pairs = [(even, odd)[pair // 4][2 + 2 * (pair % 4) : 4 + 2 * (pair % 4)] for pair in range(8)]
        here = jnp.concatenate([jnp.where(first_row, a, pltpu.roll(b, 4, 0)) for a, b in pairs], 0)
        around = jnp.concatenate([jnp.where(first_row, pltpu.roll(a, 4, 0), b) for a, b in pairs], 0)
        along_y = weighted_lanes(here, around, weights_ref[:, 256:384])
        for pair in range(8):
            rows = along_y[8 * pair : 8 * pair + 8]
            both = rows + jnp.where(sub % 4 < 2, pltpu.roll(rows, 6, 0), pltpu.roll(rows, 2, 0))
            others = jnp.where(odd_z, pltpu.roll(both, 1, 0), pltpu.roll(both, 7, 0))
            rows = rows + (same * both + opposite * others)
            scale = chosen(odd_z, (lift_scale, 1.0 / lift_scale)) * (lift_scale if pair < 4 else 1.0 / lift_scale)
            rows = rows * scale
            energy[pair] = rows * rows if g == 0 else energy[pair] + rows * rows
            for copy in range(4):
                out_ref[place(g, copy), 8 * pair : 8 * pair + 8, :] = rows
    for pair in range(8):
        for copy in range(4):
            out_ref[place(3, copy), 8 * pair : 8 * pair + 8, :] = energy[pair]


def filter_taps(ring):
    size = ring or 32

    def lifted(s):
        for value, start in ((lift_alpha, 1), (lift_beta, 0), (lift_gamma, 1), (lift_delta, 0)):
            s = list(s)
            for i in range(start, size, 2):
                s[i] += value * (s[i - 1] + s[(i + 1) % size])
        return s

    answers = [lifted([1.0 if i == j else 0.0 for i in range(size)]) for j in range(size)]
    if ring:
        return tuple(tuple(answers[(i + d) % size][i] - (0.0 if d else 1.0) for i in (0, 1)) for d in (0, 1))
    scales = (lift_scale, 1.0 / lift_scale)
    return [tuple(answers[16 + odd + k][16 + odd] * scales[odd] for odd in (0, 1)) for k in range(5)]


def flow(own, low, high):
    return pl.pallas_call(
        flow_kernel,
        out_shape=pltpu.VMEM((16, 64, 128), jnp.float32),
        in_specs=whole(4),
        out_specs=whole(1)[0],
        scratch_shapes=[
            pltpu.VMEM((4, 40, 8, 128), jnp.float32),
            pltpu.VMEM((3, 32, 8, 128), jnp.float32),
            pltpu.VMEM((3, 32, 8, 128), jnp.float32),
            pltpu.VMEM((3, 24, 8, 128), jnp.float32),
        ],
        compiler_params=pltpu.CompilerParams(vmem_limit_bytes=VMEM_LIMIT),
        cost_estimate=cost(30_000_000, 1_000_000),
        name="flow",
    )(jnp.asarray(column_weights()), own, low, high)


def slots_kernel(first_ref, owner_ref, lower_out, place_out, rank_rows):
    bf16, f32 = jnp.bfloat16, jnp.float32
    row = lax.broadcasted_iota(jnp.int32, (128, 128), 0)
    lane = lanes_of((128, 128))
    before = jnp.concatenate([(row < lane).astype(f32), jnp.ones((128, 128), f32)], 1).astype(bf16)
    pencil = row
    base = jnp.zeros((128, 128), f32)
    for b in range(64):
        mine = owner_ref[b : b + 1, :] == pencil
        counts = jnp.dot(jnp.where(mine, 1.0, 0.0).astype(bf16), before, preferred_element_type=f32)
        ranks = jnp.where(mine, base + counts[:, 0:128], 0.0)
        rank_rows[b : b + 1, :] = jnp.sum(ranks, axis=0, keepdims=True)
        base = base + counts[:, 128:256]
    owners, ranks = owner_ref[...].astype(f32), rank_rows[...]
    for part in range(2):
        even = jnp.where(lane == 2 * (row - 64 * part), 1.0, 0.0)
        odd = jnp.where(lane == 2 * (row - 64 * part) + 1, 1.0, 0.0)
        for z in range(PLANES):
            plane = (0, 2, 1, 3)[z]
            low, high = slice(16 * plane, 16 * plane + 8), slice(16 * plane + 8, 16 * plane + 16)
            owner, rank = (
                jnp.dot(values[low], even, preferred_element_type=f32)
                + jnp.dot(values[high], odd, preferred_element_type=f32)
                for values in (owners, ranks)
            )
            owner = owner.astype(jnp.int32)
            pencil = owner // 4
            lower = jnp.where(owner % 4 == first_ref[0], pencil % 16, -1)
            lower_out[part, z, :, :] = lower.astype(f32)
            place_out[part, z, :, :] = (128 * (pencil // 16)).astype(f32) + rank


def slots(first, owner_rows):
    shape = jax.ShapeDtypeStruct((2, PLANES, 8, 128), jnp.float32)
    return pl.pallas_call(
        slots_kernel,
        out_shape=(shape, shape),
        in_specs=[pl.BlockSpec(memory_space=pltpu.SMEM)] + whole(1),
        out_specs=tuple(whole(2)),
        scratch_shapes=[pltpu.VMEM((64, 128), jnp.float32)],
        compiler_params=pltpu.CompilerParams(vmem_limit_bytes=VMEM_LIMIT),
        cost_estimate=cost(600_000_000, 100_000),
        name="slots",
    )(first, owner_rows)


def gather_kernel(table_ref, lower_ref, place_ref, out_ref):
    bf16, f32 = jnp.bfloat16, jnp.float32
    slot = lax.broadcasted_iota(jnp.int32, (256, 128), 0).astype(f32).astype(bf16)
    nothing, ones = jnp.zeros((16, 128), bf16), jnp.ones((16, 128), bf16)
    total = None
    for c in range(CHUNKS):
        for pair in range(2):
            left, right = [], []
            for z in (2 * pair, 2 * pair + 1):
                values = table_ref[c, pl.ds(z, 16, stride=4), :]
                high = values.astype(bf16)
                low = (values - high.astype(f32)).astype(bf16)
                lower, place = (
                    jnp.broadcast_to(ref[c % 2, z, c // 2 : c // 2 + 1, :], (16, 128)).astype(bf16)
                    for ref in (lower_ref, place_ref)
                )
                hits = [lower == jnp.asarray(t, bf16) for t in range(16)]
                left.append(jnp.concatenate([jnp.where(hit, x, nothing) for x in (high, low) for hit in hits], 0))
                at = [jnp.where(place == slot[16 * k : 16 * k + 16], ones, nothing) for k in range(16)]
                right.append(jnp.concatenate(at, 0))
            part = lax.dot_general(
                jnp.concatenate(left, 1),
                jnp.concatenate(right, 1),
                (((1,), (1,)), ((), ())),
                preferred_element_type=f32,
            )
            total = part if total is None else total + part
    total = total[0:256] + total[256:512]
    for upper in range(2):
        out_ref[:, upper] = total[:, 128 * upper : 128 * upper + 128].reshape(16, 16, 128)


def gather(table, lower, place):
    return pl.pallas_call(
        gather_kernel,
        out_shape=jax.ShapeDtypeStruct((16, 2, 16, 128), jnp.float32),
        in_specs=whole(3),
        out_specs=whole(1)[0],
        compiler_params=pltpu.CompilerParams(vmem_limit_bytes=VMEM_LIMIT),
        cost_estimate=cost(2_200_000_000, 1_000_000),
        name="gather",
    )(table, lower, place)


def swap(x, axes):
    return lax.all_to_all(x, axes, split_axis=0, concat_axis=0, tiled=True)


def body(flow_state, line_owner):
    own = swap(pack(flow_state[0]), BLOCK_AXES)
    blocks = lax.axis_size(LONG_AXES)
    up = [(i, (i + 1) % blocks) for i in range(blocks)]
    own, lines = lax.optimization_barrier((own, line_owner.reshape(64, 128)))
    low = lax.ppermute(own, LONG_AXES, up)
    high = lax.ppermute(own.reshape(2, 4, 2, 24, 128)[:, 0:2].reshape(8, 24, 128), LONG_AXES, [(b, a) for a, b in up])
    first = lax.axis_index("y").astype(jnp.int32).reshape(1)
    own, lower, place = lax.optimization_barrier((own, *slots(first, lines)))
    table = swap(flow(own, low, high), BLOCK_AXES)
    outgoing = gather(table, lower, place).reshape(32, 16, 128)
    record = swap(outgoing, LAST_AXES)
    record = record.reshape(16, 2, 2, 8, 128).transpose(2, 1, 0, 3, 4).reshape(2, 256, 128)
    record = jnp.roll(record, -SHIFT, 1).reshape(512, 128)
    return record[None, None]


def solution(mesh):
    split = Mesh(mesh.devices.reshape(2, 2, 2, 16, 4), ("xl", "co", "xh", "z", "y"))
    in_specs = (P(("xl", "co"), None, ("xh", "z", "y"), None), P())
    out_specs = P(("xl", "co"), ("xh", "z", "y"), None, None)
    return jax.shard_map(body, mesh=split, in_specs=in_specs, out_specs=out_specs, check_vma=False)
```
